128 devices in a mesh: group: 32 (over y, z, core), context: 4 (over x).
Axes of the slice: x: 4, y: 4, z: 4, core: 2. Of those that a mesh axis runs over, the one named last changes fastest.
Arguments:
- inputs_load: bfloat16 [4, 32, 32, 24, 4096], P('context', 'group'), may hold values from -6 to 6
- maps_load: bfloat16 [4, 32, 32, 24, 256], P('context', 'group'), may hold values from -6 to 6
- steps_load: bfloat16 [4, 32, 32, 24, 64], P('context', 'group'), may hold values from 0 to 1, as said below
- decay_rate: float32 [64], replicated, may hold values from 1 to 4
- doc_lengths: int32 [32, 4], P('group'), may hold values from 1 to 2304, 3072 in all within a row
- forget_flags: int32 [32, 4], P('group'), may hold values 0 or 1
- out_grad: bfloat16 [32, 3072, 4096], P('group', 'context'), may hold values from -6 to 6
Outputs:
- layer_out: bfloat16 [32, 3072, 4096], P('group', 'context')
- grad_inputs: bfloat16 [4, 32, 32, 24, 4096], P('context', 'group')
- grad_maps: bfloat16 [4, 32, 32, 24, 256], P('context', 'group')
- grad_steps: bfloat16 [4, 32, 32, 24, 64], P('context', 'group')
The draws below stay inside these ranges and needn't reach their ends.
Inputs may be any that keep to these rules, and one draw needn't show every extreme that they name: `doc_lengths`: each row sums to 3072; in every group one document has exactly 2304 positions. `steps_load`: positive step sizes.
All inputs are finite; a program needn't handle non-finite values. No bound on the sum of `forget_flags` on one device may be relied on, other than what follows from the above.
Results may differ from the reference program's by a relative error of at most 0.02.
Values may be sent and summed in bfloat16 or wider, within the bound.
A program may use at most 256 MiB of HBM per device.

```python
import math
from functools import partial
import jax
import jax.numpy as jnp
import numpy as np
from jax import lax

H = 64
P_SIZE = 64
N = 128
SEQ_DEV = 768
BLOCK = 256
DOCS = 4
WIDE_STRIDE_NUM = 4
BATCH_TOTAL = 32
SLICES = 4
TOKEN_SPAN = 3072
PIECE = 24


def decay_params(key, fast_share):
    key = jax.random.fold_in(key, 100)
    stochastic_seeds = jax.random.split(key, 4)
    fading_factors = jnp.exp(jax.random.uniform(stochastic_seeds[0], (H,), jnp.float32, 0.0, math.log(4.0)))
    quick = jax.random.uniform(stochastic_seeds[1], (H,), jnp.float32) < fast_share
    short_span = jnp.exp(jax.random.uniform(stochastic_seeds[2], (H,), jnp.float32, math.log(30.0), math.log(50.0)))
    long_span = TOKEN_SPAN * jnp.exp(jax.random.uniform(stochastic_seeds[3], (H,), jnp.float32, math.log(4.0), math.log(16.0)))
    return (fading_factors, jnp.where(quick, short_span, long_span))


def draw_decay_rate(key, part):
    share = 0.5
    fading_factors, spans = decay_params(key, share)
    return fading_factors


def draw_steps_load(key, part):
    share = 0.5
    fading_factors, spans = decay_params(key, share)
    key = jax.random.fold_in(key, 5)
    stochastic_seeds = jax.random.split(key, 3)
    rough = jnp.exp(jax.random.uniform(stochastic_seeds[0], (BATCH_TOTAL, TOKEN_SPAN, H), jnp.float32, math.log(0.5), math.log(2.0)))
    starting_scalar = rough / (spans * fading_factors)[None, None, :]
    spike_indices = jax.random.randint(stochastic_seeds[1], (BATCH_TOTAL, WIDE_STRIDE_NUM), 0, TOKEN_SPAN)
    nesting_tier = jax.random.uniform(stochastic_seeds[2], (BATCH_TOTAL, WIDE_STRIDE_NUM), jnp.float32, 0.22, 0.45)
    spike_matches = (jnp.arange(TOKEN_SPAN)[None, :, None] == spike_indices[:, None, :]).astype(jnp.float32)
    spike_increment = jnp.sum(spike_matches * nesting_tier[:, None, :], axis=2)
    increment_line_entries = jnp.where(spike_increment[:, :, None] > 0.0, spike_increment[:, :, None] / fading_factors[None, None, :], starting_scalar)
    loader = jnp.transpose(increment_line_entries.reshape(BATCH_TOTAL, SLICES, BATCH_TOTAL, PIECE, H), (1, 2, 0, 3, 4))
    return loader.astype(jnp.bfloat16)


def with_ends(drawn, rng, least, high):
    index_at = [jax.random.randint(jax.random.fold_in(rng, axis), (), 0, length) for axis, length in enumerate(drawn.shape)]
    widest = drawn.shape.index(max(drawn.shape))
    beside = index_at[:widest] + [(index_at[widest] + 1) % drawn.shape[widest]] + index_at[widest + 1:]
    return drawn.at[tuple(index_at)].set(least).at[tuple(beside)].set(high)


def steps_of(key, dims, cuts, low, high):
    factor_of = 1.0
    for axis_at, shards_of in cuts:
        draws = jax.random.uniform(jax.random.fold_in(jax.random.fold_in(key, 6), axis_at), (shards_of,), jnp.float32, low / len(cuts), high / len(cuts))
        factor_of = factor_of * jnp.repeat(jnp.exp(draws), dims[axis_at] // shards_of).reshape((-1,) + (1,) * (len(dims) - 1 - axis_at))
    return factor_of


def length_profile(amount, total, limit, skew):
    weights = [(1 << 20) // math.isqrt(rank ** skew) + 1 for rank in range(2, amount + 1)]
    surplus, counts = total - limit - (amount - 1), [1] * (amount - 1)
    while surplus > 0:
        movable = [i for i in range(amount - 1) if counts[i] < limit]
        whole, remaining = sum([weights[i] for i in movable]), surplus
        for i in movable:
            extra = min(limit - counts[i], max(1, remaining * weights[i] // whole), surplus)
            counts[i] = counts[i] + extra
            surplus = surplus - extra
    return np.array([limit] + counts)


def ragged(key, number_of, total, limit, lean):
    if number_of == 2:
        one = jax.random.randint(key, (), max(1, total - limit), min(limit, total - 1) + 1)
        return jnp.stack([one, total - one])
    sizes = jnp.asarray(length_profile(number_of, total, limit, lean), jnp.int32)
    twos = (number_of - 1) // 2
    source_of, receiver = sizes[1:1 + 2 * twos:2], sizes[2:2 + 2 * twos:2]
    room = jnp.minimum(source_of - 1, limit - receiver)
    passed = jax.random.randint(jax.random.fold_in(key, 1), (twos,), 0, 1 << 20) % (room + 1)
    sizes = sizes.at[1:1 + 2 * twos:2].set(source_of - passed).at[2:2 + 2 * twos:2].set(receiver + passed)
    return sizes[jax.random.permutation(jax.random.fold_in(key, 2), number_of)]


def noise(key, shape, scale, reach, cuts=(), kind=jnp.bfloat16):
    values = scale * jax.random.normal(key, shape, jnp.float32)
    if cuts:
        values = values * steps_of(key, shape, cuts, -0.22, 0.18)
    return jnp.clip(values, -reach, reach).astype(kind)


def setup_inputs(seed: int = 0) -> dict:
    arg_keys = jax.random.split(jax.random.key(seed), 8)
    return {
        "inputs_load": noise(arg_keys[0], (SLICES, BATCH_TOTAL, BATCH_TOTAL, PIECE, H * P_SIZE), 1.0, 6.0, ((0, 4), (1, 32))),
        "maps_load": noise(arg_keys[1], (SLICES, BATCH_TOTAL, BATCH_TOTAL, PIECE, 2 * N), (2 * N ** -0.25), 6.0, ((0, 4), (1, 32))),
        "steps_load": draw_steps_load(jax.random.fold_in(arg_keys[7], 71), 0),
        "decay_rate": draw_decay_rate(jax.random.fold_in(arg_keys[7], 71), 0),
        "doc_lengths": jax.vmap(lambda own: ragged(own, DOCS, TOKEN_SPAN, 3 * SEQ_DEV, 2))(jax.random.split(arg_keys[4], BATCH_TOTAL)).reshape((BATCH_TOTAL, DOCS)).astype(jnp.int32),
        "forget_flags": with_ends((jax.random.randint(arg_keys[5], (BATCH_TOTAL, DOCS), 0, 2) < 1).astype(jnp.int32), jax.random.fold_in(arg_keys[5], 1), 0, 1),
        "out_grad": noise(arg_keys[6], (BATCH_TOTAL, TOKEN_SPAN, H * P_SIZE), 1.0, 6.0, ((0, 32), (1, 4))),
    }


def segment_ids(lengths, positions):
    doc_ends = jnp.cumsum(lengths).astype(jnp.int32)
    return lax.optimization_barrier(jnp.sum((positions[:, None] >= doc_ends[None, :]).astype(jnp.int32), axis=1)).astype(jnp.int32)

def token_weight(segment, flag_row):
    doc_index = jnp.arange(flag_row.shape[0], dtype=jnp.int32)
    picked = lax.optimization_barrier(jnp.sum(jnp.where(segment[:, None] == doc_index[None, :], flag_row[None, :], 0), axis=1))
    return 1.0 - 1.5 * picked.astype(jnp.float32)

def block_step(fading_factors, carried_in, pieces):
    old_state, previous = carried_in
    x_block, map_block, step_block, seg_block = pieces
    row_count = x_block.shape[0]
    head_count = fading_factors.shape[0]
    map_width = map_block.shape[1] // 2
    values = x_block.astype(jnp.bfloat16).reshape(row_count, head_count, -1)
    b_part = map_block[:, :map_width].astype(jnp.bfloat16)
    c_part = map_block[:, map_width:].astype(jnp.bfloat16)
    cumulative = jnp.cumsum(-step_block * fading_factors[None, :], axis=0).T
    row_index = jnp.arange(row_count)
    kept_mask = (seg_block[:, None] == seg_block[None, :]) & (row_index[:, None] >= row_index[None, :])
    spread = cumulative[:, :, None] - cumulative[:, None, :]
    decay_table = jnp.where(kept_mask[None], jnp.exp(jnp.where(kept_mask[None], spread, 0.0)), 0.0)
    scores = jnp.dot(c_part, b_part.T, preferred_element_type=jnp.float32)
    mixing = (decay_table * scores[None] * step_block.T[:, None, :]).astype(jnp.bfloat16)
    inner_out = jnp.einsum('hij,jhp->ihp', mixing, values, preferred_element_type=jnp.float32)
    opening = jnp.where((seg_block == previous)[None, :], jnp.exp(cumulative), 0.0)
    state_copy = old_state.astype(jnp.bfloat16)
    carried = jnp.einsum('in,hpn->ihp', c_part, state_copy, preferred_element_type=jnp.float32) * opening.T[:, :, None]
    last_seg = seg_block[row_count - 1]
    tail_weight = jnp.where((seg_block == last_seg)[None, :], jnp.exp(cumulative[:, row_count - 1:] - cumulative), 0.0) * step_block.T
    tail = (tail_weight.T[:, :, None] * values.astype(jnp.float32)).astype(jnp.bfloat16)
    fresh_state = jnp.einsum('jhp,jn->hpn', tail, b_part, preferred_element_type=jnp.float32)
    through = jnp.where(last_seg == previous, jnp.exp(cumulative[:, row_count - 1]), 0.0)
    new_state = fresh_state + through[:, None, None] * old_state
    return ((new_state, last_seg), (inner_out + carried).reshape(row_count, -1))

def run_blocks(values, map_rows, increment_line_entries, fading_factors, segment, first_state, previous):
    row_count = values.shape[0]
    blocks = row_count // BLOCK
    pieces = (values.reshape(blocks, BLOCK, -1), map_rows.reshape(blocks, BLOCK, -1), increment_line_entries.reshape(blocks, BLOCK, -1), segment.reshape(blocks, BLOCK))
    stepper = jax.checkpoint(partial(block_step, fading_factors))
    (final_state, last_seg), outputs = lax.scan(stepper, (first_state, previous), pieces)
    return (outputs.reshape(row_count, -1), final_state)

def reference(inputs_load, maps_load, steps_load, decay_rate, doc_lengths, forget_flags, out_grad):

    def to_groups(loader):
        return jnp.transpose(loader, (2, 0, 1, 3, 4)).reshape(BATCH_TOTAL, TOKEN_SPAN, loader.shape[-1])

    def to_loader(grouped):
        return jnp.transpose(grouped.reshape(BATCH_TOTAL, SLICES, BATCH_TOTAL, PIECE, grouped.shape[-1]), (1, 2, 0, 3, 4))
    positions = jnp.arange(TOKEN_SPAN, dtype=jnp.int32)
    start_state = jnp.zeros((H, P_SIZE, N), jnp.float32)
    no_segment = jnp.asarray(-1, jnp.int32)

    def one_group(items):
        values, map_rows, increment_line_entries, lengths, flag_row, cotangent = items
        segment = segment_ids(lengths, positions)

        def forward(values, map_rows, increment_line_entries):
            return run_blocks(values, map_rows, increment_line_entries, decay_rate, segment, start_state, no_segment)[0]
        outputs, pullback = jax.vjp(forward, values, map_rows.astype(jnp.float32), increment_line_entries.astype(jnp.float32))
        weighted = cotangent.astype(jnp.float32) * token_weight(segment, flag_row)[:, None]
        grad_values, grad_rows, grad_sizes = pullback(weighted)
        return (outputs.astype(jnp.bfloat16), grad_values.astype(jnp.bfloat16), grad_rows.astype(jnp.bfloat16), grad_sizes.astype(jnp.bfloat16))
    layer_out, grad_inputs, grad_maps, grad_steps = lax.map(one_group, (to_groups(inputs_load), to_groups(maps_load), to_groups(steps_load), doc_lengths, forget_flags, out_grad))
    return (layer_out, to_loader(grad_inputs), to_loader(grad_maps), to_loader(grad_steps))
```

```python
from functools import partial
from types import SimpleNamespace

import jax
import jax.numpy as jnp
from jax import lax
from jax.experimental import pallas as pl
from jax.experimental.pallas import tpu as pltpu
from jax.sharding import PartitionSpec as P

BLOCK = 128
CHUNK_HEADS = 8
AHEAD = 3
LANES = 128
LOG2E = 1.4426950408889634
MESH = pl.DeviceIdType.MESH
F32 = jnp.float32
BF16 = jnp.bfloat16


def dot_nn(a, b):
    return jnp.dot(a, b, preferred_element_type=F32)


def dot_nt(a, b):
    return lax.dot_general(a, b, (((1,), (1,)), ((), ())), preferred_element_type=F32)


def dot_tn(a, b):
    return lax.dot_general(a, b, (((0,), (0,)), ((), ())), preferred_element_type=F32)


def dot_exact(a, b):
    return jnp.dot(a, b, precision=lax.Precision.HIGHEST, preferred_element_type=F32)


def halves(a):
    high = a.astype(BF16)
    return jnp.concatenate([high, (a - high.astype(F32)).astype(BF16)], axis=1)


def loop(count, body):
    def step(i, carry):
        body(i)
        return carry

    lax.fori_loop(0, count, step, 0)


def kernel(dims, names, *refs):
    r = SimpleNamespace(**dict(zip(names, refs)))
    groups, slices, piece, heads, size = dims
    seq = groups * piece
    blocks = seq // BLOCK
    chunks = heads // CHUNK_HEADS
    width = CHUNK_HEADS * size
    docs = r.lens.shape[1]
    me, place = lax.axis_index("group"), lax.axis_index("context")
    offset = place * seq

    def peer(i):
        return lax.rem(me + i, groups)

    def ctx(i):
        return lax.rem(place + i, slices)

    def rows(b):
        return pl.ds(pl.multiple_of(b * BLOCK, BLOCK), BLOCK)

    def cols(k):
        return pl.ds(pl.multiple_of(k * width, width), width)

    def piece_rows(j):
        return pl.ds(pl.multiple_of(j * piece, 8), piece)

    def to_group(src, dst, send, recv, j):
        return pltpu.make_async_remote_copy(
            src_ref=src, dst_ref=dst, send_sem=send, recv_sem=recv,
            device_id={"group": j}, device_id_type=MESH,
        )

    def to_context(src, dst, send, recv, c):
        return pltpu.make_async_remote_copy(
            src_ref=src, dst_ref=dst, send_sem=send, recv_sem=recv,
            device_id={"context": c}, device_id_type=MESH,
        )

    def take(ref, sem):
        pltpu.make_async_copy(ref, ref, sem).wait()

    barrier = pltpu.get_barrier_semaphore()

    def greet_group(i):
        pl.semaphore_signal(barrier, inc=1, device_id={"group": peer(i + 1)}, device_id_type=MESH)

    def greet_context(i):
        pl.semaphore_signal(barrier, inc=1, device_id={"context": ctx(i + 1)}, device_id_type=MESH)

    loop(groups - 1, greet_group)
    loop(slices - 1, greet_context)
    pl.semaphore_wait(barrier, groups + slices - 2)

    def send_side(i):
        j = peer(i + 1)
        to_group(r.side_hbm.at[j], r.side.at[me], r.side_send.at[0], r.side_recv.at[0], j).start()

    def own_side():
        return pltpu.make_async_copy(r.side_hbm.at[me], r.side.at[me], r.side_own.at[0])

    def send_values(k):
        def one(i):
            j = peer(i + 1)
            to_group(
                r.x_hbm.at[j, :, cols(k)], r.vals.at[k, me], r.val_send.at[k], r.val_recv.at[k], j
            ).start()

        loop(groups - 1, one)
        own_values(k).start()

    def own_values(k):
        return pltpu.make_async_copy(
            r.x_hbm.at[me, :, cols(k)], r.vals.at[k, me], r.val_own.at[k]
        )

    def load_grad(k):
        slot = lax.rem(k, 3)
        return pltpu.make_async_copy(r.og_hbm.at[:, cols(k)], r.og.at[slot], r.og_sem.at[slot])

    def store_out(k):
        slot = lax.rem(k, 2)
        return pltpu.make_async_copy(r.y.at[slot], r.y_hbm.at[:, cols(k)], r.y_sem.at[slot])

    loop(groups - 1, send_side)
    own_side().start()
    loop(min(AHEAD, chunks), send_values)
    load_grad(0).start()

    take(r.side.at[pl.ds(0, groups - 1)], r.side_recv.at[0])
    own_side().wait()

    def unpack_side(j):
        r.sidef[piece_rows(j), :] = r.side[j].astype(F32)

    loop(groups, unpack_side)

    ends = [r.lens[0, 0]]
    for d in range(1, docs):
        ends.append(ends[-1] + r.lens[0, d])

    def segment(position):
        return sum(jnp.where(position >= end, 1, 0) for end in ends)

    row_at = lax.broadcasted_iota(jnp.int32, (BLOCK, BLOCK), 0)
    col_at = lax.broadcasted_iota(jnp.int32, (BLOCK, BLOCK), 1)
    rate = r.rate[0:1, :]

    def block_segments(b):
        first = offset + b * BLOCK
        before = jnp.where(first > 0, segment(first - 1), -1)
        last = segment(first + BLOCK - 1)
        return segment(first + row_at), segment(first + col_at), before, last

    def prepare(b):
        seg_row, seg_col, before, last = block_segments(b)
        kept = (seg_row == seg_col) & (row_at >= col_at)
        r.mask[b] = jnp.where(kept, 0.0, -1e30)
        part = r.sidef[rows(b), :]
        b_map, c_map, step = part[:, :LANES], part[:, LANES : 2 * LANES], part[:, 2 * LANES :]
        b_part, c_part = b_map.astype(BF16), c_map.astype(BF16)
        r.b_map[b], r.c_map[b] = b_part, c_part
        r.b_turned[b], r.c_turned[b] = b_map.T.astype(BF16), c_map.T.astype(BF16)
        r.scores[b] = dot_nt(c_part, b_part)
        r.step[b] = step.astype(BF16)
        lower = jnp.where(row_at >= col_at, 1.0, 0.0)
        cum = dot_exact(lower, step * (rate * -LOG2E))
        end = cum[BLOCK - 1 : BLOCK, :]
        r.opening[b] = halves(jnp.where(seg_row == before, jnp.exp2(cum), 0.0))
        r.tail[b] = halves(jnp.where(seg_row == last, jnp.exp2(end - cum), 0.0))
        r.through[pl.ds(b, 1), :] = jnp.where(last == before, jnp.exp2(end), 0.0)
        for k in range(chunks):
            r.cum_col[b, k] = cum[:, k * CHUNK_HEADS : (k + 1) * CHUNK_HEADS]
        r.cum_row[b] = cum.T
        picked = sum(jnp.where(seg_row == d, r.flags[0, d], 0) for d in range(docs))
        r.weight[b] = 1.0 - 1.5 * picked.astype(F32)
        r.dscores[b] = jnp.zeros((BLOCK, BLOCK), F32)
        for name in ("dc", "db", "edge", "dstep"):
            getattr(r, name)[b] = jnp.zeros((BLOCK, LANES), F32)

    r.through[...] = jnp.ones(r.through.shape, F32)
    r.flow[...] = jnp.zeros(r.flow.shape, F32)
    loop(blocks, prepare)

    decay = r.through[0:1, :]
    for b in range(1, blocks):
        decay = decay * r.through[b : b + 1, :]
    r.decay_own[...] = jnp.broadcast_to(decay, r.decay_own.shape)

    def send_decay(i):
        c = ctx(i + 1)
        to_context(
            r.decay_own, r.decays.at[place], r.decay_send.at[0], r.decay_recv.at[0], c
        ).start()

    loop(slices - 1, send_decay)
    take(r.decays.at[pl.ds(0, slices - 1)], r.decay_recv.at[0])
    take(r.decays.at[pl.ds(0, slices - 1)], r.decay_send.at[0])

    def spread(k):
        head = lax.broadcasted_iota(jnp.int32, (LANES, width), 0)
        col = lax.broadcasted_iota(jnp.int32, (LANES, width), 1)
        low = (head - k * CHUNK_HEADS) * size
        return jnp.where((col >= low) & (col < low + size), 1.0, 0.0).astype(BF16)

    def first_half(k):
        slot, held = lax.rem(k, 2), lax.rem(k, 3)
        take(r.vals.at[k, pl.ds(0, groups - 1)], r.val_recv.at[k])
        own_values(k).wait()
        load_grad(k).wait()

        def unpack(j):
            r.x[slot, piece_rows(j), :] = r.vals[k, j].astype(F32)

        loop(groups, unpack)
        one = spread(k)
        r.one[slot, pl.ds(0, LANES)] = one
        r.one[slot, pl.ds(LANES, LANES)] = one
        r.through_wide[slot] = dot_nn(halves(r.through[...]), r.one[slot])
        r.run[...] = jnp.zeros(r.run.shape, F32)

        def fresh(b):
            both = r.one[slot]
            step = dot_nn(r.step[b], both[:LANES])
            tail = dot_nn(r.tail[b], both)
            scaled = (r.x[slot, rows(b), :] * step * tail).astype(BF16)
            r.fresh[slot, b] = dot_nn(r.b_turned[b], scaled)
            through = r.through_wide[slot, pl.ds(b, 1), :]
            r.run[...] = through * r.run[...] + r.fresh[slot, b]
            opening = dot_nn(r.opening[b], both)
            grad = r.og[held, rows(b), :].astype(F32) * r.weight[b][:, :1]
            r.og[held, rows(b), :] = grad.astype(BF16)
            r.dfresh[slot, b] = dot_nn(r.c_turned[b], (grad * opening).astype(BF16))

        loop(blocks, fresh)
        r.states[k, 0] = r.run[...].astype(BF16)
        r.run[...] = jnp.zeros(r.run.shape, F32)

        def back(turn):
            b = blocks - 1 - turn
            through = r.through_wide[slot, pl.ds(b, 1), :]
            r.run[...] = through * r.run[...] + r.dfresh[slot, b]

        loop(blocks, back)
        r.states[k, 1] = r.run[...].astype(BF16)

        def send_state(i):
            c = ctx(i + 1)
            kind = jnp.where(c > place, 0, 1)
            to_context(
                r.states.at[k, kind], r.around.at[k, place], r.state_send.at[k], r.state_recv.at[k], c
            ).start()

        loop(slices - 1, send_state)

    def second_half(k):
        slot, held = lax.rem(k, 2), lax.rem(k, 3)
        take(r.around.at[k, pl.ds(0, slices - 1)], r.state_recv.at[k])

        def widened(c):
            return dot_nn(halves(r.decays[c]), r.one[slot])[:1]

        r.run[...] = jnp.zeros(r.run.shape, F32)

        def enter(c):
            @pl.when(c < place)
            def _():
                r.run[...] = r.around[k, c].astype(F32) + widened(c) * r.run[...]

        loop(slices, enter)

        def forward(b):
            r.state[b] = r.run[...].astype(BF16)
            through = r.through_wide[slot, pl.ds(b, 1), :]
            new = through * r.run[...] + r.fresh[slot, b]
            r.run[...] = new
            r.fresh[slot, b] = new

        loop(blocks, forward)
        r.run[...] = jnp.zeros(r.run.shape, F32)

        def leave(turn):
            c = slices - 1 - turn

            @pl.when(c > place)
            def _():
                r.run[...] = r.around[k, c].astype(F32) + widened(c) * r.run[...]

        loop(slices, leave)
        r.flow_wide[...] = jnp.zeros(r.flow_wide.shape, F32)

        def backward(turn):
            b = blocks - 1 - turn
            now = r.run[...]
            r.dstate[b] = now.astype(BF16)
            r.flow_wide[pl.ds(b, 1), :] = jnp.sum(now * r.fresh[slot, b], axis=0, keepdims=True)
            through = r.through_wide[slot, pl.ds(b, 1), :]
            r.run[...] = through * now + r.dfresh[slot, b]

        loop(blocks, backward)
        one = r.one[slot, pl.ds(0, LANES)]

        def per_head(a):
            high = a.astype(BF16)
            low = (a - high.astype(F32)).astype(BF16)
            return dot_nt(high, one) + dot_nt(low, one)

        r.flow[...] += per_head(r.flow_wide[...])

        @pl.when(k >= 2)
        def _():
            store_out(k - 2).wait()

        lane = lax.broadcasted_iota(jnp.int32, (1, LANES), 1)
        left = jnp.where(lane < size, 1.0, 0.0).astype(BF16)
        right = jnp.where(lane < size, 0.0, 1.0).astype(BF16)

        def block(b):
            both = r.one[slot]
            x = r.x[slot, rows(b), :]
            step = dot_nn(r.step[b], both[:LANES])
            tail = dot_nn(r.tail[b], both)
            opening = dot_nn(r.opening[b], both)
            grad = r.og[held, rows(b), :]
            stepped = x * step
            xd = stepped.astype(BF16)
            state, dstate = r.state[b], r.dstate[b]
            carried = dot_nn(r.c_map[b], state) * opening
            r.dc[b] += dot_nt((grad.astype(F32) * opening).astype(BF16), state)
            r.db[b] += dot_nt((stepped * tail).astype(BF16), dstate)
            dtail = dot_nn(r.b_map[b], dstate) * tail
            mask, scores = r.mask[b], r.scores[b]
            cum_row = r.cum_row[b, pl.ds(pl.multiple_of(k * CHUNK_HEADS, 8), CHUNK_HEADS), :]
            cum_col = r.cum_col[b, k]
            dscores = r.dscores[b]
            ys, dxs = [], []
            for p in range(width // LANES):
                at = slice(p * LANES, (p + 1) * LANES)
                xp, gp = xd[:, at], grad[:, at]
                x_two = jnp.concatenate([xp * left, xp * right], axis=0)
                g_two = jnp.concatenate([gp * left, gp * right], axis=0)
                dmixing = dot_nt(gp, x_two)
                mixing = []
                for q in range(2):
                    h = 2 * p + q
                    fade = jnp.exp2(cum_col[:, h : h + 1] - cum_row[h : h + 1, :] + mask)
                    mixing.append((fade * scores).astype(BF16))
                    dscores = dscores + dmixing[:, q * BLOCK : (q + 1) * BLOCK] * fade
                ys.append(dot_nn(jnp.concatenate(mixing, axis=1), x_two))
                dxs.append(dot_tn(jnp.concatenate(mixing, axis=0), g_two))
            r.dscores[b] = dscores
            y = jnp.concatenate(ys, axis=1) + carried
            dxd = jnp.concatenate(dxs, axis=1) + dtail
            r.y[slot, rows(b), :] = y.astype(BF16)
            r.gx[rows(b), :] = dxd * step
            r.edge[b] += per_head(grad.astype(F32) * y - xd.astype(F32) * dxd)
            r.dstep[b] += per_head(x * dxd)

        loop(blocks, block)
        store_out(k).start()

        def give(i):
            j = peer(i)
            r.gsend[k, j] = r.gx[piece_rows(j), :].astype(BF16)

            @pl.when(i > 0)
            def _():
                to_group(
                    r.gsend.at[k, j], r.gx_hbm.at[me, :, cols(k)], r.gx_send.at[k], r.gx_recv.at[k], j
                ).start()

        loop(groups, give)
        own_gradient(k).start()

    def own_gradient(k):
        return pltpu.make_async_copy(
            r.gsend.at[k, me], r.gx_hbm.at[me, :, cols(k)], r.gx_own.at[k]
        )

    def turn(k):
        @pl.when(k + AHEAD < chunks)
        def _():
            send_values(k + AHEAD)

        @pl.when(k < chunks)
        def _():
            @pl.when(k + 1 < chunks)
            def _():
                load_grad(k + 1).start()

            first_half(k)

        @pl.when(k > 0)
        def _():
            second_half(k - 1)

    loop(chunks + 1, turn)

    def finish(b):
        seg_row, seg_col, before, last = block_segments(b)
        dscores = r.dscores[b].astype(BF16)
        later = jnp.where((seg_row == seg_col) & (col_at >= row_at), 1.0, 0.0)
        dlog = dot_exact(later, r.edge[b])
        dlog = dlog + jnp.where(seg_row == last, r.flow[pl.ds(b, 1), :], 0.0)
        r.sidef[rows(b), pl.ds(0, LANES)] = r.db[b] + dot_tn(dscores, r.c_map[b])
        r.sidef[rows(b), pl.ds(LANES, LANES)] = r.dc[b] + dot_nn(dscores, r.b_map[b])
        r.sidef[rows(b), pl.ds(2 * LANES, LANES)] = r.dstep[b] - rate * dlog

    loop(blocks, finish)

    def give_side(i):
        j = peer(i)
        r.gside[j] = r.sidef[piece_rows(j), :].astype(BF16)

        @pl.when(i > 0)
        def _():
            to_group(
                r.gside.at[j], r.gside_hbm.at[me], r.gside_send.at[0], r.gside_recv.at[0], j
            ).start()

    loop(groups, give_side)
    own = pltpu.make_async_copy(r.gside.at[me], r.gside_hbm.at[me], r.gside_own.at[0])
    own.start()

    def settle(k):
        take(r.vals.at[k, pl.ds(0, groups - 1)], r.val_send.at[k])
        take(r.around.at[k, pl.ds(0, slices - 1)], r.state_send.at[k])
        take(r.vals.at[k, pl.ds(0, groups - 1)], r.gx_send.at[k])
        take(r.vals.at[k, pl.ds(0, groups - 1)], r.gx_recv.at[k])
        own_gradient(k).wait()

    loop(chunks, settle)
    for k in range(max(chunks - 2, 0), chunks):
        store_out(k).wait()
    own.wait()
    for sem in (r.side_send, r.gside_send, r.gside_recv):
        take(r.side.at[pl.ds(0, groups - 1)], sem.at[0])


def on_device(inputs_load, maps_load, steps_load, decay_rate, doc_lengths, forget_flags, out_grad):
    groups, slices = lax.axis_size("group"), lax.axis_size("context")
    heads = decay_rate.shape[0]
    piece, total = inputs_load.shape[3:]
    size = total // heads
    seq = groups * piece
    blocks = seq // BLOCK
    chunks = heads // CHUNK_HEADS
    width = CHUNK_HEADS * size
    fill = LANES - heads
    side = jnp.concatenate(
        [maps_load, steps_load, jnp.zeros(steps_load.shape[:-1] + (fill,), BF16)], axis=-1
    ).reshape(groups, piece, 3 * LANES)
    rate = jnp.broadcast_to(jnp.pad(decay_rate, (0, fill))[None], (8, LANES))

    dma = pltpu.SemaphoreType.DMA
    vmem = pltpu.VMEM
    scratch = dict(
        vals=vmem((chunks, groups, piece, width), BF16),
        gsend=vmem((chunks, groups, piece, width), BF16),
        side=vmem((groups, piece, 3 * LANES), BF16),
        gside=vmem((groups, piece, 3 * LANES), BF16),
        sidef=vmem((seq, 3 * LANES), F32),
        og=vmem((3, seq, width), BF16),
        y=vmem((2, seq, width), BF16),
        x=vmem((2, seq, width), F32),
        gx=vmem((seq, width), F32),
        one=vmem((2, 2 * LANES, width), BF16),
        fresh=vmem((2, blocks, LANES, width), F32),
        dfresh=vmem((2, blocks, LANES, width), F32),
        state=vmem((blocks, LANES, width), BF16),
        dstate=vmem((blocks, LANES, width), BF16),
        run=vmem((LANES, width), F32),
        states=vmem((chunks, 2, LANES, width), BF16),
        around=vmem((chunks, slices, LANES, width), BF16),
        decays=vmem((slices, 8, LANES), F32),
        decay_own=vmem((8, LANES), F32),
        through=vmem((8, LANES), F32),
        through_wide=vmem((2, 8, width), F32),
        flow=vmem((8, LANES), F32),
        flow_wide=vmem((8, width), F32),
        mask=vmem((blocks, BLOCK, BLOCK), F32),
        scores=vmem((blocks, BLOCK, BLOCK), F32),
        dscores=vmem((blocks, BLOCK, BLOCK), F32),
        weight=vmem((blocks, BLOCK, BLOCK), F32),
        b_map=vmem((blocks, BLOCK, LANES), BF16),
        c_map=vmem((blocks, BLOCK, LANES), BF16),
        b_turned=vmem((blocks, LANES, BLOCK), BF16),
        c_turned=vmem((blocks, LANES, BLOCK), BF16),
        step=vmem((blocks, BLOCK, LANES), BF16),
        opening=vmem((blocks, BLOCK, 2 * LANES), BF16),
        tail=vmem((blocks, BLOCK, 2 * LANES), BF16),
        cum_col=vmem((blocks, chunks, BLOCK, CHUNK_HEADS), F32),
        cum_row=vmem((blocks, LANES, BLOCK), F32),
        dc=vmem((blocks, BLOCK, LANES), F32),
        db=vmem((blocks, BLOCK, LANES), F32),
        edge=vmem((blocks, BLOCK, LANES), F32),
        dstep=vmem((blocks, BLOCK, LANES), F32),
        side_send=dma((1,)), side_recv=dma((1,)), side_own=dma((1,)),
        gside_send=dma((1,)), gside_recv=dma((1,)), gside_own=dma((1,)),
        decay_send=dma((1,)), decay_recv=dma((1,)),
        val_send=dma((chunks,)), val_recv=dma((chunks,)), val_own=dma((chunks,)),
        gx_send=dma((chunks,)), gx_recv=dma((chunks,)), gx_own=dma((chunks,)),
        state_send=dma((chunks,)), state_recv=dma((chunks,)),
        og_sem=dma((3,)), y_sem=dma((2,)),
    )
    names = (
        "x_hbm", "side_hbm", "og_hbm", "rate", "lens", "flags", "y_hbm", "gx_hbm", "gside_hbm",
    ) + tuple(scratch)
    anywhere = pl.BlockSpec(memory_space=pl.ANY)
    in_vmem = pl.BlockSpec(memory_space=pltpu.VMEM)
    in_smem = pl.BlockSpec(memory_space=pltpu.SMEM)
    y, gx, gside = pl.pallas_call(
        partial(kernel, (groups, slices, piece, heads, size), names),
        out_shape=(
            jax.ShapeDtypeStruct((seq, total), BF16),
            jax.ShapeDtypeStruct((groups, piece, total), BF16),
            jax.ShapeDtypeStruct((groups, piece, 3 * LANES), BF16),
        ),
        in_specs=[anywhere, anywhere, anywhere, in_vmem, in_smem, in_smem],
        out_specs=[anywhere, anywhere, anywhere],
        scratch_shapes=list(scratch.values()),
        compiler_params=pltpu.CompilerParams(
            collective_id=0, has_side_effects=True, vmem_limit_bytes=60 * 1024 * 1024
        ),
        name="layer",
    )(
        inputs_load.reshape(groups, piece, total), side, out_grad[0], rate, doc_lengths, forget_flags
    )
    gside = gside[None, None]
    return (
        y[None],
        gx[None, None],
        gside[..., : 2 * LANES],
        gside[..., 2 * LANES : 2 * LANES + heads],
    )


def solution(mesh):
    in_specs = (
        P("context", "group", None, None, None),
        P("context", "group", None, None, None),
        P("context", "group", None, None, None),
        P(),
        P("group", None),
        P("group", None),
        P("group", "context", None),
    )
    out_specs = (
        P("group", "context", None),
        P("context", "group", None, None, None),
        P("context", "group", None, None, None),
        P("context", "group", None, None, None),
    )
    return jax.shard_map(
        on_device, mesh=mesh, in_specs=in_specs, out_specs=out_specs, check_vma=False
    )
```

```python
from functools import partial
from types import SimpleNamespace

import jax
import jax.numpy as jnp
from jax import lax
from jax.experimental import pallas as pl
from jax.experimental.pallas import tpu as pltpu
from jax.sharding import PartitionSpec as P

BLOCK = 128
CHUNK_HEADS = 8
AHEAD = 3
LANES = 128
LOG2E = 1.4426950408889634
MESH = pl.DeviceIdType.MESH
F32 = jnp.float32
BF16 = jnp.bfloat16


def dot_nn(a, b):
    return jnp.dot(a, b, preferred_element_type=F32)


def dot_nt(a, b):
    return lax.dot_general(a, b, (((1,), (1,)), ((), ())), preferred_element_type=F32)


def dot_tn(a, b):
    return lax.dot_general(a, b, (((0,), (0,)), ((), ())), preferred_element_type=F32)


def dot_exact(a, b):
    return jnp.dot(a, b, precision=lax.Precision.HIGHEST, preferred_element_type=F32)


def halves(a):
    high = a.astype(BF16)
    return jnp.concatenate([high, (a - high.astype(F32)).astype(BF16)], axis=1)


def loop(count, body):
    def step(i, carry):
        body(i)
        return carry

    lax.fori_loop(0, count, step, 0)


def kernel(dims, names, *refs):
    r = SimpleNamespace(**dict(zip(names, refs)))
    groups, slices, piece, heads, size = dims
    seq = groups * piece
    blocks = seq // BLOCK
    chunks = heads // CHUNK_HEADS
    width = CHUNK_HEADS * size
    docs = r.lens.shape[1]
    me, place = lax.axis_index("group"), lax.axis_index("context")
    offset = place * seq

    def peer(i):
        return lax.rem(me + i, groups)

    turns = ((0, 1), (1, 0), (0, 3), (3, 0), (0, 2), (2, 0), (1, 1), (3, 3), (1, 3), (3, 1))
    turns += ((2, 2), (1, 2), (2, 1), (3, 2), (2, 3))

    def others():
        if groups != 32:
            return [peer(i) for i in range(1, groups)]
        core, z, y = lax.rem(me, 2), lax.rem(me // 2, 4), me // 8
        found = []
        for other in (0, 1):
            for dy, dz in turns:
                chip = lax.rem(y + dy, 4) * 4 + lax.rem(z + dz, 4)
                found.append(chip * 2 + lax.rem(core + other, 2))
        return found + [me + 1 - 2 * core]

    def ctx(i):
        return lax.rem(place + i, slices)

    def rows(b):
        return pl.ds(pl.multiple_of(b * BLOCK, BLOCK), BLOCK)

    def cols(k):
        return pl.ds(pl.multiple_of(k * width, width), width)

    def piece_rows(j):
        return pl.ds(pl.multiple_of(j * piece, 8), piece)

    def to_group(src, dst, send, recv, j):
        return pltpu.make_async_remote_copy(
            src_ref=src, dst_ref=dst, send_sem=send, recv_sem=recv,
            device_id={"group": j}, device_id_type=MESH,
        )

    def to_context(src, dst, send, recv, c):
        return pltpu.make_async_remote_copy(
            src_ref=src, dst_ref=dst, send_sem=send, recv_sem=recv,
            device_id={"context": c}, device_id_type=MESH,
        )

    def take(ref, sem):
        pltpu.make_async_copy(ref, ref, sem).wait()

    barrier = pltpu.get_barrier_semaphore()

    def greet_group(i):
        pl.semaphore_signal(barrier, inc=1, device_id={"group": peer(i + 1)}, device_id_type=MESH)

    def greet_context(i):
        pl.semaphore_signal(barrier, inc=1, device_id={"context": ctx(i + 1)}, device_id_type=MESH)

    loop(groups - 1, greet_group)
    loop(slices - 1, greet_context)
    pl.semaphore_wait(barrier, groups + slices - 2)

    def send_side(j):
        to_group(r.side_hbm.at[j], r.side.at[me], r.side_send.at[0], r.side_recv.at[0], j).start()

    def own_side():
        return pltpu.make_async_copy(r.side_hbm.at[me], r.side.at[me], r.side_own.at[0])

    def send_values(k):
        for j in others():
            to_group(
                r.x_hbm.at[j, :, cols(k)], r.vals.at[k, me], r.val_send.at[k], r.val_recv.at[k], j
            ).start()
        own_values(k).start()

    def own_values(k):
        return pltpu.make_async_copy(
            r.x_hbm.at[me, :, cols(k)], r.vals.at[k, me], r.val_own.at[k]
        )

    def load_grad(k):
        slot = lax.rem(k, 3)
        return pltpu.make_async_copy(r.og_hbm.at[:, cols(k)], r.og.at[slot], r.og_sem.at[slot])

    def store_out(k):
        slot = lax.rem(k, 2)
        return pltpu.make_async_copy(r.y.at[slot], r.y_hbm.at[:, cols(k)], r.y_sem.at[slot])

    for j in others():
        send_side(j)
    own_side().start()
    loop(min(AHEAD, chunks), send_values)
    load_grad(0).start()

    take(r.side.at[pl.ds(0, groups - 1)], r.side_recv.at[0])
    own_side().wait()

    def unpack_side(j):
        r.sidef[piece_rows(j), :] = r.side[j].astype(F32)

    loop(groups, unpack_side)

    ends = [r.lens[0, 0]]
    for d in range(1, docs):
        ends.append(ends[-1] + r.lens[0, d])

    def segment(position):
        return sum(jnp.where(position >= end, 1, 0) for end in ends)

    row_at = lax.broadcasted_iota(jnp.int32, (BLOCK, BLOCK), 0)
    col_at = lax.broadcasted_iota(jnp.int32, (BLOCK, BLOCK), 1)
    rate = r.rate[0:1, :]

    def block_segments(b):
        first = offset + b * BLOCK
        before = jnp.where(first > 0, segment(first - 1), -1)
        last = segment(first + BLOCK - 1)
        return segment(first + row_at), segment(first + col_at), before, last

    def prepare(b):
        seg_row, seg_col, before, last = block_segments(b)
        kept = (seg_row == seg_col) & (row_at >= col_at)
        r.mask[b] = jnp.where(kept, 0.0, -1e30)
        part = r.sidef[rows(b), :]
        b_map, c_map, step = part[:, :LANES], part[:, LANES : 2 * LANES], part[:, 2 * LANES :]
        b_part, c_part = b_map.astype(BF16), c_map.astype(BF16)
        r.b_map[b], r.c_map[b] = b_part, c_part
        r.b_turned[b], r.c_turned[b] = b_map.T.astype(BF16), c_map.T.astype(BF16)
        r.scores[b] = dot_nt(c_part, b_part)
        r.step[b] = step.astype(BF16)
        lower = jnp.where(row_at >= col_at, 1.0, 0.0)
        cum = dot_exact(lower, step * (rate * -LOG2E))
        end = cum[BLOCK - 1 : BLOCK, :]
        r.opening[b] = halves(jnp.where(seg_row == before, jnp.exp2(cum), 0.0))
        r.tail[b] = halves(jnp.where(seg_row == last, jnp.exp2(end - cum), 0.0))
        r.through[pl.ds(b, 1), :] = jnp.where(last == before, jnp.exp2(end), 0.0)
        for k in range(chunks):
            r.cum_col[b, k] = cum[:, k * CHUNK_HEADS : (k + 1) * CHUNK_HEADS]
        r.cum_row[b] = cum.T
        picked = sum(jnp.where(seg_row == d, r.flags[0, d], 0) for d in range(docs))
        r.weight[b] = 1.0 - 1.5 * picked.astype(F32)
        r.dscores[b] = jnp.zeros((BLOCK, BLOCK), F32)
        for name in ("dc", "db", "edge", "dstep"):
            getattr(r, name)[b] = jnp.zeros((BLOCK, LANES), F32)

    r.through[...] = jnp.ones(r.through.shape, F32)
    r.flow[...] = jnp.zeros(r.flow.shape, F32)
    loop(blocks, prepare)

    decay = r.through[0:1, :]
    for b in range(1, blocks):
        decay = decay * r.through[b : b + 1, :]
    r.decay_own[...] = jnp.broadcast_to(decay, r.decay_own.shape)

    def send_decay(i):
        c = ctx(i + 1)
        to_context(
            r.decay_own, r.decays.at[place], r.decay_send.at[0], r.decay_recv.at[0], c
        ).start()

    loop(slices - 1, send_decay)
    take(r.decays.at[pl.ds(0, slices - 1)], r.decay_recv.at[0])
    take(r.decays.at[pl.ds(0, slices - 1)], r.decay_send.at[0])

    def spread(k):
        head = lax.broadcasted_iota(jnp.int32, (LANES, width), 0)
        col = lax.broadcasted_iota(jnp.int32, (LANES, width), 1)
        low = (head - k * CHUNK_HEADS) * size
        return jnp.where((col >= low) & (col < low + size), 1.0, 0.0).astype(BF16)

    def first_half(k):
        slot, held = lax.rem(k, 2), lax.rem(k, 3)
        take(r.vals.at[k, pl.ds(0, groups - 1)], r.val_recv.at[k])
        own_values(k).wait()
        load_grad(k).wait()

        def unpack(j):
            r.x[slot, piece_rows(j), :] = r.vals[k, j].astype(F32)

        loop(groups, unpack)
        one = spread(k)
        r.one[slot, pl.ds(0, LANES)] = one
        r.one[slot, pl.ds(LANES, LANES)] = one
        r.through_wide[slot] = dot_nn(halves(r.through[...]), r.one[slot])
        r.run[...] = jnp.zeros(r.run.shape, F32)

        def fresh(b):
            both = r.one[slot]
            step = dot_nn(r.step[b], both[:LANES])
            tail = dot_nn(r.tail[b], both)
            scaled = (r.x[slot, rows(b), :] * step * tail).astype(BF16)
            r.fresh[slot, b] = dot_nn(r.b_turned[b], scaled)
            through = r.through_wide[slot, pl.ds(b, 1), :]
            r.run[...] = through * r.run[...] + r.fresh[slot, b]
            opening = dot_nn(r.opening[b], both)
            grad = r.og[held, rows(b), :].astype(F32) * r.weight[b][:, :1]
            r.og[held, rows(b), :] = grad.astype(BF16)
            r.dfresh[slot, b] = dot_nn(r.c_turned[b], (grad * opening).astype(BF16))

        loop(blocks, fresh)
        r.states[k, 0] = r.run[...].astype(BF16)
        r.run[...] = jnp.zeros(r.run.shape, F32)

        def back(turn):
            b = blocks - 1 - turn
            through = r.through_wide[slot, pl.ds(b, 1), :]
            r.run[...] = through * r.run[...] + r.dfresh[slot, b]

        loop(blocks, back)
        r.states[k, 1] = r.run[...].astype(BF16)

        def send_state(i):
            c = ctx(i + 1)
            kind = jnp.where(c > place, 0, 1)
            to_context(
                r.states.at[k, kind], r.around.at[k, place], r.state_send.at[k], r.state_recv.at[k], c
            ).start()

        loop(slices - 1, send_state)

    def second_half(k):
        slot, held = lax.rem(k, 2), lax.rem(k, 3)
        take(r.around.at[k, pl.ds(0, slices - 1)], r.state_recv.at[k])

        def widened(c):
            return dot_nn(halves(r.decays[c]), r.one[slot])[:1]

        r.run[...] = jnp.zeros(r.run.shape, F32)

        def enter(c):
            @pl.when(c < place)
            def _():
                r.run[...] = r.around[k, c].astype(F32) + widened(c) * r.run[...]

        loop(slices, enter)

        def forward(b):
            r.state[b] = r.run[...].astype(BF16)
            through = r.through_wide[slot, pl.ds(b, 1), :]
            new = through * r.run[...] + r.fresh[slot, b]
            r.run[...] = new
            r.fresh[slot, b] = new

        loop(blocks, forward)
        r.run[...] = jnp.zeros(r.run.shape, F32)

        def leave(turn):
            c = slices - 1 - turn

            @pl.when(c > place)
            def _():
                r.run[...] = r.around[k, c].astype(F32) + widened(c) * r.run[...]

        loop(slices, leave)
        r.flow_wide[...] = jnp.zeros(r.flow_wide.shape, F32)

        def backward(turn):
            b = blocks - 1 - turn
            now = r.run[...]
            r.dstate[b] = now.astype(BF16)
            r.flow_wide[pl.ds(b, 1), :] = jnp.sum(now * r.fresh[slot, b], axis=0, keepdims=True)
            through = r.through_wide[slot, pl.ds(b, 1), :]
            r.run[...] = through * now + r.dfresh[slot, b]

        loop(blocks, backward)
        one = r.one[slot, pl.ds(0, LANES)]

        def per_head(a):
            high = a.astype(BF16)
            low = (a - high.astype(F32)).astype(BF16)
            return dot_nt(high, one) + dot_nt(low, one)

        r.flow[...] += per_head(r.flow_wide[...])

        @pl.when(k >= 2)
        def _():
            store_out(k - 2).wait()

        lane = lax.broadcasted_iota(jnp.int32, (1, LANES), 1)
        left = jnp.where(lane < size, 1.0, 0.0).astype(BF16)
        right = jnp.where(lane < size, 0.0, 1.0).astype(BF16)

        def block(b):
            both = r.one[slot]
            x = r.x[slot, rows(b), :]
            step = dot_nn(r.step[b], both[:LANES])
            tail = dot_nn(r.tail[b], both)
            opening = dot_nn(r.opening[b], both)
            grad = r.og[held, rows(b), :]
            stepped = x * step
            xd = stepped.astype(BF16)
            state, dstate = r.state[b], r.dstate[b]
            carried = dot_nn(r.c_map[b], state) * opening
            r.dc[b] += dot_nt((grad.astype(F32) * opening).astype(BF16), state)
            r.db[b] += dot_nt((stepped * tail).astype(BF16), dstate)
            dtail = dot_nn(r.b_map[b], dstate) * tail
            mask, scores = r.mask[b], r.scores[b]
            cum_row = r.cum_row[b, pl.ds(pl.multiple_of(k * CHUNK_HEADS, 8), CHUNK_HEADS), :]
            cum_col = r.cum_col[b, k]
            dscores = r.dscores[b]
            ys, dxs = [], []
            for p in range(width // LANES):
                at = slice(p * LANES, (p + 1) * LANES)
                xp, gp = xd[:, at], grad[:, at]
                x_two = jnp.concatenate([xp * left, xp * right], axis=0)
                g_two = jnp.concatenate([gp * left, gp * right], axis=0)
                dmixing = dot_nt(gp, x_two)
                mixing = []
                for q in range(2):
                    h = 2 * p + q
                    fade = jnp.exp2(cum_col[:, h : h + 1] - cum_row[h : h + 1, :] + mask)
                    mixing.append((fade * scores).astype(BF16))
                    dscores = dscores + dmixing[:, q * BLOCK : (q + 1) * BLOCK] * fade
                ys.append(dot_nn(jnp.concatenate(mixing, axis=1), x_two))
                dxs.append(dot_tn(jnp.concatenate(mixing, axis=0), g_two))
            r.dscores[b] = dscores
            y = jnp.concatenate(ys, axis=1) + carried
            dxd = jnp.concatenate(dxs, axis=1) + dtail
            r.y[slot, rows(b), :] = y.astype(BF16)
            r.gx[rows(b), :] = dxd * step
            r.edge[b] += per_head(grad.astype(F32) * y - xd.astype(F32) * dxd)
            r.dstep[b] += per_head(x * dxd)

        loop(blocks, block)
        store_out(k).start()

        def pack(j):
            r.gsend[k, j] = r.gx[piece_rows(j), :].astype(BF16)

        for j in others():
            pack(j)
            to_group(
                r.gsend.at[k, j], r.gx_hbm.at[me, :, cols(k)], r.gx_send.at[k], r.gx_recv.at[k], j
            ).start()
        pack(me)
        own_gradient(k).start()

    def own_gradient(k):
        return pltpu.make_async_copy(
            r.gsend.at[k, me], r.gx_hbm.at[me, :, cols(k)], r.gx_own.at[k]
        )

    def turn(k):
        @pl.when(k + AHEAD < chunks)
        def _():
            send_values(k + AHEAD)

        @pl.when(k < chunks)
        def _():
            @pl.when(k + 1 < chunks)
            def _():
                load_grad(k + 1).start()

            first_half(k)

        @pl.when(k > 0)
        def _():
            second_half(k - 1)

    loop(chunks + 1, turn)

    def finish(b):
        seg_row, seg_col, before, last = block_segments(b)
        dscores = r.dscores[b].astype(BF16)
        later = jnp.where((seg_row == seg_col) & (col_at >= row_at), 1.0, 0.0)
        dlog = dot_exact(later, r.edge[b])
        dlog = dlog + jnp.where(seg_row == last, r.flow[pl.ds(b, 1), :], 0.0)
        r.sidef[rows(b), pl.ds(0, LANES)] = r.db[b] + dot_tn(dscores, r.c_map[b])
        r.sidef[rows(b), pl.ds(LANES, LANES)] = r.dc[b] + dot_nn(dscores, r.b_map[b])
        r.sidef[rows(b), pl.ds(2 * LANES, LANES)] = r.dstep[b] - rate * dlog

    loop(blocks, finish)

    def pack_side(j):
        r.gside[j] = r.sidef[piece_rows(j), :].astype(BF16)

    for j in others():
        pack_side(j)
        to_group(
            r.gside.at[j], r.gside_hbm.at[me], r.gside_send.at[0], r.gside_recv.at[0], j
        ).start()
    pack_side(me)
    own = pltpu.make_async_copy(r.gside.at[me], r.gside_hbm.at[me], r.gside_own.at[0])
    own.start()

    def settle(k):
        take(r.vals.at[k, pl.ds(0, groups - 1)], r.val_send.at[k])
        take(r.around.at[k, pl.ds(0, slices - 1)], r.state_send.at[k])
        take(r.vals.at[k, pl.ds(0, groups - 1)], r.gx_send.at[k])
        take(r.vals.at[k, pl.ds(0, groups - 1)], r.gx_recv.at[k])
        own_gradient(k).wait()

    loop(chunks, settle)
    for k in range(max(chunks - 2, 0), chunks):
        store_out(k).wait()
    own.wait()
    for sem in (r.side_send, r.gside_send, r.gside_recv):
        take(r.side.at[pl.ds(0, groups - 1)], sem.at[0])


def on_device(inputs_load, maps_load, steps_load, decay_rate, doc_lengths, forget_flags, out_grad):
    groups, slices = lax.axis_size("group"), lax.axis_size("context")
    heads = decay_rate.shape[0]
    piece, total = inputs_load.shape[3:]
    size = total // heads
    seq = groups * piece
    blocks = seq // BLOCK
    chunks = heads // CHUNK_HEADS
    width = CHUNK_HEADS * size
    fill = LANES - heads
    side = jnp.concatenate(
        [maps_load, steps_load, jnp.zeros(steps_load.shape[:-1] + (fill,), BF16)], axis=-1
    ).reshape(groups, piece, 3 * LANES)
    rate = jnp.broadcast_to(jnp.pad(decay_rate, (0, fill))[None], (8, LANES))

    dma = pltpu.SemaphoreType.DMA
    vmem = pltpu.VMEM
    scratch = dict(
        vals=vmem((chunks, groups, piece, width), BF16),
        gsend=vmem((chunks, groups, piece, width), BF16),
        side=vmem((groups, piece, 3 * LANES), BF16),
        gside=vmem((groups, piece, 3 * LANES), BF16),
        sidef=vmem((seq, 3 * LANES), F32),
        og=vmem((3, seq, width), BF16),
        y=vmem((2, seq, width), BF16),
        x=vmem((2, seq, width), F32),
        gx=vmem((seq, width), F32),
        one=vmem((2, 2 * LANES, width), BF16),
        fresh=vmem((2, blocks, LANES, width), F32),
        dfresh=vmem((2, blocks, LANES, width), F32),
        state=vmem((blocks, LANES, width), BF16),
        dstate=vmem((blocks, LANES, width), BF16),
        run=vmem((LANES, width), F32),
        states=vmem((chunks, 2, LANES, width), BF16),
        around=vmem((chunks, slices, LANES, width), BF16),
        decays=vmem((slices, 8, LANES), F32),
        decay_own=vmem((8, LANES), F32),
        through=vmem((8, LANES), F32),
        through_wide=vmem((2, 8, width), F32),
        flow=vmem((8, LANES), F32),
        flow_wide=vmem((8, width), F32),
        mask=vmem((blocks, BLOCK, BLOCK), F32),
        scores=vmem((blocks, BLOCK, BLOCK), F32),
        dscores=vmem((blocks, BLOCK, BLOCK), F32),
        weight=vmem((blocks, BLOCK, BLOCK), F32),
        b_map=vmem((blocks, BLOCK, LANES), BF16),
        c_map=vmem((blocks, BLOCK, LANES), BF16),
        b_turned=vmem((blocks, LANES, BLOCK), BF16),
        c_turned=vmem((blocks, LANES, BLOCK), BF16),
        step=vmem((blocks, BLOCK, LANES), BF16),
        opening=vmem((blocks, BLOCK, 2 * LANES), BF16),
        tail=vmem((blocks, BLOCK, 2 * LANES), BF16),
        cum_col=vmem((blocks, chunks, BLOCK, CHUNK_HEADS), F32),
        cum_row=vmem((blocks, LANES, BLOCK), F32),
        dc=vmem((blocks, BLOCK, LANES), F32),
        db=vmem((blocks, BLOCK, LANES), F32),
        edge=vmem((blocks, BLOCK, LANES), F32),
        dstep=vmem((blocks, BLOCK, LANES), F32),
        side_send=dma((1,)), side_recv=dma((1,)), side_own=dma((1,)),
        gside_send=dma((1,)), gside_recv=dma((1,)), gside_own=dma((1,)),
        decay_send=dma((1,)), decay_recv=dma((1,)),
        val_send=dma((chunks,)), val_recv=dma((chunks,)), val_own=dma((chunks,)),
        gx_send=dma((chunks,)), gx_recv=dma((chunks,)), gx_own=dma((chunks,)),
        state_send=dma((chunks,)), state_recv=dma((chunks,)),
        og_sem=dma((3,)), y_sem=dma((2,)),
    )
    names = (
        "x_hbm", "side_hbm", "og_hbm", "rate", "lens", "flags", "y_hbm", "gx_hbm", "gside_hbm",
    ) + tuple(scratch)
    anywhere = pl.BlockSpec(memory_space=pl.ANY)
    in_vmem = pl.BlockSpec(memory_space=pltpu.VMEM)
    in_smem = pl.BlockSpec(memory_space=pltpu.SMEM)
    y, gx, gside = pl.pallas_call(
        partial(kernel, (groups, slices, piece, heads, size), names),
        out_shape=(
            jax.ShapeDtypeStruct((seq, total), BF16),
            jax.ShapeDtypeStruct((groups, piece, total), BF16),
            jax.ShapeDtypeStruct((groups, piece, 3 * LANES), BF16),
        ),
        in_specs=[anywhere, anywhere, anywhere, in_vmem, in_smem, in_smem],
        out_specs=[anywhere, anywhere, anywhere],
        scratch_shapes=list(scratch.values()),
        compiler_params=pltpu.CompilerParams(
            collective_id=0, has_side_effects=True, vmem_limit_bytes=60 * 1024 * 1024
        ),
        name="layer",
    )(
        inputs_load.reshape(groups, piece, total), side, out_grad[0], rate, doc_lengths, forget_flags
    )
    gside = gside[None, None]
    return (
        y[None],
        gx[None, None],
        gside[..., : 2 * LANES],
        gside[..., 2 * LANES : 2 * LANES + heads],
    )


def solution(mesh):
    in_specs = (
        P("context", "group", None, None, None),
        P("context", "group", None, None, None),
        P("context", "group", None, None, None),
        P(),
        P("group", None),
        P("group", None),
        P("group", "context", None),
    )
    out_specs = (
        P("group", "context", None),
        P("context", "group", None, None, None),
        P("context", "group", None, None, None),
        P("context", "group", None, None, None),
    )
    return jax.shard_map(
        on_device, mesh=mesh, in_specs=in_specs, out_specs=out_specs, check_vma=False
    )
```

```python
from functools import partial
from types import SimpleNamespace

import jax
import jax.numpy as jnp
from jax import lax
from jax.experimental import pallas as pl
from jax.experimental.pallas import tpu as pltpu
from jax.sharding import PartitionSpec as P

BLOCK = 128
CHUNK_HEADS = 8
AHEAD = 3
LANES = 128
LOG2E = 1.4426950408889634
MESH = pl.DeviceIdType.MESH
F32 = jnp.float32
BF16 = jnp.bfloat16


def dot_nn(a, b):
    return jnp.dot(a, b, preferred_element_type=F32)


def dot_nt(a, b):
    return lax.dot_general(a, b, (((1,), (1,)), ((), ())), preferred_element_type=F32)


def dot_tn(a, b):
    return lax.dot_general(a, b, (((0,), (0,)), ((), ())), preferred_element_type=F32)


def dot_exact(a, b):
    return jnp.dot(a, b, precision=lax.Precision.HIGHEST, preferred_element_type=F32)


def halves(a):
    high = a.astype(BF16)
    return jnp.concatenate([high, (a - high.astype(F32)).astype(BF16)], axis=1)


def loop(count, body):
    def step(i, carry):
        body(i)
        return carry

    lax.fori_loop(0, count, step, 0)


def kernel(dims, names, *refs):
    r = SimpleNamespace(**dict(zip(names, refs)))
    groups, slices, piece, heads, size = dims
    seq = groups * piece
    blocks = seq // BLOCK
    chunks = heads // CHUNK_HEADS
    width = CHUNK_HEADS * size
    docs = r.lens.shape[1]
    me, place = lax.axis_index("group"), lax.axis_index("context")
    offset = place * seq

    def peer(i):
        return lax.rem(me + i, groups)

    turns = ((0, 1), (1, 0), (0, 3), (3, 0), (0, 2), (2, 0), (1, 1), (3, 3), (1, 3), (3, 1))
    turns += ((2, 2), (1, 2), (2, 1), (3, 2), (2, 3))

    def others():
        if groups != 32:
            return [peer(i) for i in range(1, groups)]
        core, z, y = lax.rem(me, 2), lax.rem(me // 2, 4), me // 8
        found = []
        for other in (0, 1):
            for dy, dz in turns:
                chip = lax.rem(y + dy, 4) * 4 + lax.rem(z + dz, 4)
                found.append(chip * 2 + lax.rem(core + other, 2))
        return found + [me + 1 - 2 * core]

    def ctx(i):
        return lax.rem(place + i, slices)

    def rows(b):
        return pl.ds(pl.multiple_of(b * BLOCK, BLOCK), BLOCK)

    def cols(k):
        return pl.ds(pl.multiple_of(k * width, width), width)

    def piece_rows(j):
        return pl.ds(pl.multiple_of(j * piece, 8), piece)

    def to_group(src, dst, send, recv, j):
        return pltpu.make_async_remote_copy(
            src_ref=src, dst_ref=dst, send_sem=send, recv_sem=recv,
            device_id={"group": j}, device_id_type=MESH,
        )

    def to_context(src, dst, send, recv, c):
        return pltpu.make_async_remote_copy(
            src_ref=src, dst_ref=dst, send_sem=send, recv_sem=recv,
            device_id={"context": c}, device_id_type=MESH,
        )

    def take(ref, sem):
        pltpu.make_async_copy(ref, ref, sem).wait()

    barrier = pltpu.get_barrier_semaphore()

    def greet_group(i):
        pl.semaphore_signal(barrier, inc=1, device_id={"group": peer(i + 1)}, device_id_type=MESH)

    def greet_context(i):
        pl.semaphore_signal(barrier, inc=1, device_id={"context": ctx(i + 1)}, device_id_type=MESH)

    loop(groups - 1, greet_group)
    loop(slices - 1, greet_context)
    pl.semaphore_wait(barrier, groups + slices - 2)

    side_refs = ((r.maps_hbm, r.maps), (r.steps_hbm, r.steps))

    def send_side(j):
        for n, (source, target) in enumerate(side_refs):
            to_group(
                source.at[j], target.at[me], r.side_send.at[n], r.side_recv.at[n], j
            ).start()

    def own_side():
        return [
            pltpu.make_async_copy(source.at[me], target.at[me], r.side_own.at[n])
            for n, (source, target) in enumerate(side_refs)
        ]

    def send_values(k):
        for j in others():
            to_group(
                r.x_hbm.at[j, :, cols(k)], r.vals.at[k, me], r.val_send.at[k], r.val_recv.at[k], j
            ).start()
        own_values(k).start()

    def own_values(k):
        return pltpu.make_async_copy(
            r.x_hbm.at[me, :, cols(k)], r.vals.at[k, me], r.val_own.at[k]
        )

    def load_grad(k):
        slot = lax.rem(k, 3)
        return pltpu.make_async_copy(r.og_hbm.at[:, cols(k)], r.og.at[slot], r.og_sem.at[slot])

    def store_out(k):
        slot = lax.rem(k, 2)
        return pltpu.make_async_copy(r.y.at[slot], r.y_hbm.at[:, cols(k)], r.y_sem.at[slot])

    for j in others():
        send_side(j)
    for copy in own_side():
        copy.start()
    loop(min(AHEAD, chunks), send_values)
    load_grad(0).start()

    for n, (_, target) in enumerate(side_refs):
        take(target.at[pl.ds(0, groups - 1)], r.side_recv.at[n])
    for copy in own_side():
        copy.wait()
    step_at = slice(2 * LANES, 2 * LANES + heads)
    r.sidef[:, 2 * LANES :] = jnp.zeros((seq, LANES), F32)

    def unpack_side(j):
        r.sidef[piece_rows(j), : 2 * LANES] = r.maps[j].astype(F32)
        r.sidef[piece_rows(j), step_at] = r.steps[j].astype(F32)

    loop(groups, unpack_side)

    ends = [r.lens[0, 0]]
    for d in range(1, docs):
        ends.append(ends[-1] + r.lens[0, d])

    def segment(position):
        return sum(jnp.where(position >= end, 1, 0) for end in ends)

    row_at = lax.broadcasted_iota(jnp.int32, (BLOCK, BLOCK), 0)
    col_at = lax.broadcasted_iota(jnp.int32, (BLOCK, BLOCK), 1)
    rate = r.rate[...]
    if heads < LANES:
        rate = jnp.concatenate([rate, jnp.zeros((1, LANES - heads), F32)], axis=1)

    def block_segments(b):
        first = offset + b * BLOCK
        before = jnp.where(first > 0, segment(first - 1), -1)
        last = segment(first + BLOCK - 1)
        return segment(first + row_at), segment(first + col_at), before, last

    def prepare(b):
        seg_row, seg_col, before, last = block_segments(b)
        kept = (seg_row == seg_col) & (row_at >= col_at)
        r.mask[b] = jnp.where(kept, 0.0, -1e30)
        part = r.sidef[rows(b), :]
        b_map, c_map, step = part[:, :LANES], part[:, LANES : 2 * LANES], part[:, 2 * LANES :]
        b_part, c_part = b_map.astype(BF16), c_map.astype(BF16)
        r.b_map[b], r.c_map[b] = b_part, c_part
        r.b_turned[b], r.c_turned[b] = b_map.T.astype(BF16), c_map.T.astype(BF16)
        r.scores[b] = dot_nt(c_part, b_part)
        r.step[b] = step.astype(BF16)
        lower = jnp.where(row_at >= col_at, 1.0, 0.0)
        cum = dot_exact(lower, step * (rate * -LOG2E))
        end = cum[BLOCK - 1 : BLOCK, :]
        r.opening[b] = halves(jnp.where(seg_row == before, jnp.exp2(cum), 0.0))
        r.tail[b] = halves(jnp.where(seg_row == last, jnp.exp2(end - cum), 0.0))
        r.through[pl.ds(b, 1), :] = jnp.where(last == before, jnp.exp2(end), 0.0)
        for k in range(chunks):
            r.cum_col[b, k] = cum[:, k * CHUNK_HEADS : (k + 1) * CHUNK_HEADS]
        r.cum_row[b] = cum.T
        picked = sum(jnp.where(seg_row == d, r.flags[0, d], 0) for d in range(docs))
        r.weight[b] = 1.0 - 1.5 * picked.astype(F32)
        r.dscores[b] = jnp.zeros((BLOCK, BLOCK), F32)
        for name in ("dc", "db", "edge", "dstep"):
            getattr(r, name)[b] = jnp.zeros((BLOCK, LANES), F32)

    r.through[...] = jnp.ones(r.through.shape, F32)
    r.flow[...] = jnp.zeros(r.flow.shape, F32)
    loop(blocks, prepare)

    decay = r.through[0:1, :]
    for b in range(1, blocks):
        decay = decay * r.through[b : b + 1, :]
    r.decay_own[...] = jnp.broadcast_to(decay, r.decay_own.shape)

    def send_decay(i):
        c = ctx(i + 1)
        to_context(
            r.decay_own, r.decays.at[place], r.decay_send.at[0], r.decay_recv.at[0], c
        ).start()

    loop(slices - 1, send_decay)
    take(r.decays.at[pl.ds(0, slices - 1)], r.decay_recv.at[0])
    take(r.decays.at[pl.ds(0, slices - 1)], r.decay_send.at[0])

    def spread(k):
        head = lax.broadcasted_iota(jnp.int32, (LANES, width), 0)
        col = lax.broadcasted_iota(jnp.int32, (LANES, width), 1)
        low = (head - k * CHUNK_HEADS) * size
        return jnp.where((col >= low) & (col < low + size), 1.0, 0.0).astype(BF16)

    def first_half(k):
        slot, held = lax.rem(k, 2), lax.rem(k, 3)
        take(r.vals.at[k, pl.ds(0, groups - 1)], r.val_recv.at[k])
        own_values(k).wait()
        load_grad(k).wait()

        def unpack(j):
            r.x[slot, piece_rows(j), :] = r.vals[k, j].astype(F32)

        loop(groups, unpack)
        one = spread(k)
        r.one[slot, pl.ds(0, LANES)] = one
        r.one[slot, pl.ds(LANES, LANES)] = one
        r.through_wide[slot] = dot_nn(halves(r.through[...]), r.one[slot])
        r.run[...] = jnp.zeros(r.run.shape, F32)

        def fresh(b):
            both = r.one[slot]
            step = dot_nn(r.step[b], both[:LANES])
            tail = dot_nn(r.tail[b], both)
            scaled = (r.x[slot, rows(b), :] * step * tail).astype(BF16)
            r.fresh[slot, b] = dot_nn(r.b_turned[b], scaled)
            through = r.through_wide[slot, pl.ds(b, 1), :]
            r.run[...] = through * r.run[...] + r.fresh[slot, b]
            opening = dot_nn(r.opening[b], both)
            grad = r.og[held, rows(b), :].astype(F32) * r.weight[b][:, :1]
            r.og[held, rows(b), :] = grad.astype(BF16)
            r.dfresh[slot, b] = dot_nn(r.c_turned[b], (grad * opening).astype(BF16))

        loop(blocks, fresh)
        r.states[k, 0] = r.run[...].astype(BF16)
        r.run[...] = jnp.zeros(r.run.shape, F32)

        def back(turn):
            b = blocks - 1 - turn
            through = r.through_wide[slot, pl.ds(b, 1), :]
            r.run[...] = through * r.run[...] + r.dfresh[slot, b]

        loop(blocks, back)
        r.states[k, 1] = r.run[...].astype(BF16)

        def send_state(i):
            c = ctx(i + 1)
            kind = jnp.where(c > place, 0, 1)
            to_context(
                r.states.at[k, kind], r.around.at[k, place], r.state_send.at[k], r.state_recv.at[k], c
            ).start()

        loop(slices - 1, send_state)

    def second_half(k):
        slot, held = lax.rem(k, 2), lax.rem(k, 3)
        take(r.around.at[k, pl.ds(0, slices - 1)], r.state_recv.at[k])

        def widened(c):
            return dot_nn(halves(r.decays[c]), r.one[slot])[:1]

        r.run[...] = jnp.zeros(r.run.shape, F32)

        def enter(c):
            @pl.when(c < place)
            def _():
                r.run[...] = r.around[k, c].astype(F32) + widened(c) * r.run[...]

        loop(slices, enter)

        def forward(b):
            r.state[b] = r.run[...].astype(BF16)
            through = r.through_wide[slot, pl.ds(b, 1), :]
            new = through * r.run[...] + r.fresh[slot, b]
            r.run[...] = new
            r.fresh[slot, b] = new

        loop(blocks, forward)
        r.run[...] = jnp.zeros(r.run.shape, F32)

        def leave(turn):
            c = slices - 1 - turn

            @pl.when(c > place)
            def _():
                r.run[...] = r.around[k, c].astype(F32) + widened(c) * r.run[...]

        loop(slices, leave)
        r.flow_wide[...] = jnp.zeros(r.flow_wide.shape, F32)

        def backward(turn):
            b = blocks - 1 - turn
            now = r.run[...]
            r.dstate[b] = now.astype(BF16)
            r.flow_wide[pl.ds(b, 1), :] = jnp.sum(now * r.fresh[slot, b], axis=0, keepdims=True)
            through = r.through_wide[slot, pl.ds(b, 1), :]
            r.run[...] = through * now + r.dfresh[slot, b]

        loop(blocks, backward)
        one = r.one[slot, pl.ds(0, LANES)]

        def per_head(a):
            high = a.astype(BF16)
            low = (a - high.astype(F32)).astype(BF16)
            return dot_nt(high, one) + dot_nt(low, one)

        r.flow[...] += per_head(r.flow_wide[...])

        @pl.when(k >= 2)
        def _():
            store_out(k - 2).wait()

        lane = lax.broadcasted_iota(jnp.int32, (1, LANES), 1)
        left = jnp.where(lane < size, 1.0, 0.0).astype(BF16)
        right = jnp.where(lane < size, 0.0, 1.0).astype(BF16)

        def block(b):
            both = r.one[slot]
            x = r.x[slot, rows(b), :]
            step = dot_nn(r.step[b], both[:LANES])
            tail = dot_nn(r.tail[b], both)
            opening = dot_nn(r.opening[b], both)
            grad = r.og[held, rows(b), :]
            stepped = x * step
            xd = stepped.astype(BF16)
            state, dstate = r.state[b], r.dstate[b]
            carried = dot_nn(r.c_map[b], state) * opening
            r.dc[b] += dot_nt((grad.astype(F32) * opening).astype(BF16), state)
            r.db[b] += dot_nt((stepped * tail).astype(BF16), dstate)
            dtail = dot_nn(r.b_map[b], dstate) * tail
            mask, scores = r.mask[b], r.scores[b]
            cum_row = r.cum_row[b, pl.ds(pl.multiple_of(k * CHUNK_HEADS, 8), CHUNK_HEADS), :]
            cum_col = r.cum_col[b, k]
            dscores = r.dscores[b]
            ys, dxs = [], []
            for p in range(width // LANES):
                at = slice(p * LANES, (p + 1) * LANES)
                xp, gp = xd[:, at], grad[:, at]
                x_two = jnp.concatenate([xp * left, xp * right], axis=0)
                g_two = jnp.concatenate([gp * left, gp * right], axis=0)
                dmixing = dot_nt(gp, x_two)
                mixing = []
                for q in range(2):
                    h = 2 * p + q
                    fade = jnp.exp2(cum_col[:, h : h + 1] - cum_row[h : h + 1, :] + mask)
                    mixing.append((fade * scores).astype(BF16))
                    dscores = dscores + dmixing[:, q * BLOCK : (q + 1) * BLOCK] * fade
                ys.append(dot_nn(jnp.concatenate(mixing, axis=1), x_two))
                dxs.append(dot_tn(jnp.concatenate(mixing, axis=0), g_two))
            r.dscores[b] = dscores
            y = jnp.concatenate(ys, axis=1) + carried
            dxd = jnp.concatenate(dxs, axis=1) + dtail
            r.y[slot, rows(b), :] = y.astype(BF16)
            r.gx[rows(b), :] = dxd * step
            r.edge[b] += per_head(grad.astype(F32) * y - xd.astype(F32) * dxd)
            r.dstep[b] += per_head(x * dxd)

        loop(blocks, block)
        store_out(k).start()

        def pack(j):
            r.gsend[k, j] = r.gx[piece_rows(j), :].astype(BF16)

        for j in others():
            pack(j)
            to_group(
                r.gsend.at[k, j], r.gx_hbm.at[me, :, cols(k)], r.gx_send.at[k], r.gx_recv.at[k], j
            ).start()
        pack(me)
        own_gradient(k).start()

    def own_gradient(k):
        return pltpu.make_async_copy(
            r.gsend.at[k, me], r.gx_hbm.at[me, :, cols(k)], r.gx_own.at[k]
        )

    def turn(k):
        @pl.when(k + AHEAD < chunks)
        def _():
            send_values(k + AHEAD)

        @pl.when(k < chunks)
        def _():
            @pl.when(k + 1 < chunks)
            def _():
                load_grad(k + 1).start()

            first_half(k)

        @pl.when(k > 0)
        def _():
            second_half(k - 1)

    loop(chunks + 1, turn)

    def finish(b):
        seg_row, seg_col, before, last = block_segments(b)
        dscores = r.dscores[b].astype(BF16)
        later = jnp.where((seg_row == seg_col) & (col_at >= row_at), 1.0, 0.0)
        dlog = dot_exact(later, r.edge[b])
        dlog = dlog + jnp.where(seg_row == last, r.flow[pl.ds(b, 1), :], 0.0)
        r.sidef[rows(b), pl.ds(0, LANES)] = r.db[b] + dot_tn(dscores, r.c_map[b])
        r.sidef[rows(b), pl.ds(LANES, LANES)] = r.dc[b] + dot_nn(dscores, r.b_map[b])
        r.sidef[rows(b), pl.ds(2 * LANES, LANES)] = r.dstep[b] - rate * dlog

    loop(blocks, finish)

    gside_refs = ((r.gmaps, r.gmaps_hbm), (r.gsteps, r.gsteps_hbm))

    def pack_side(j):
        r.gmaps[j] = r.sidef[piece_rows(j), : 2 * LANES].astype(BF16)
        r.gsteps[j] = r.sidef[piece_rows(j), step_at].astype(BF16)

    for j in others():
        pack_side(j)
        for n, (source, target) in enumerate(gside_refs):
            to_group(
                source.at[j], target.at[me], r.gside_send.at[n], r.gside_recv.at[n], j
            ).start()
    pack_side(me)
    own = [
        pltpu.make_async_copy(source.at[me], target.at[me], r.gside_own.at[n])
        for n, (source, target) in enumerate(gside_refs)
    ]
    for copy in own:
        copy.start()

    def settle(k):
        take(r.vals.at[k, pl.ds(0, groups - 1)], r.val_send.at[k])
        take(r.around.at[k, pl.ds(0, slices - 1)], r.state_send.at[k])
        take(r.vals.at[k, pl.ds(0, groups - 1)], r.gx_send.at[k])
        take(r.vals.at[k, pl.ds(0, groups - 1)], r.gx_recv.at[k])
        own_gradient(k).wait()

    loop(chunks, settle)
    for k in range(max(chunks - 2, 0), chunks):
        store_out(k).wait()
    for copy in own:
        copy.wait()
    for sem in (r.side_send, r.gside_send, r.gside_recv):
        for n, (_, like) in enumerate(side_refs):
            take(like.at[pl.ds(0, groups - 1)], sem.at[n])


COPY_PARTS = 8


def hand_over(*refs):
    count = len(refs) // 2
    sems = refs[-1]
    copies = []
    for n, (source, target) in enumerate(zip(refs[:count], refs[count : 2 * count])):
        length = source.shape[0] // COPY_PARTS
        for p in range(COPY_PARTS):
            at = pl.ds(p * length, length)
            copies.append(pltpu.make_async_copy(source.at[at], target.at[at], sems.at[n, p]))
    for copy in copies:
        copy.start()
    for copy in copies:
        copy.wait()


def on_device(inputs_load, maps_load, steps_load, decay_rate, doc_lengths, forget_flags, out_grad):
    groups, slices = lax.axis_size("group"), lax.axis_size("context")
    heads = decay_rate.shape[0]
    piece, total = inputs_load.shape[3:]
    size = total // heads
    seq = groups * piece
    blocks = seq // BLOCK
    chunks = heads // CHUNK_HEADS
    width = CHUNK_HEADS * size

    dma = pltpu.SemaphoreType.DMA
    vmem = pltpu.VMEM
    scratch = dict(
        vals=vmem((chunks, groups, piece, width), BF16),
        gsend=vmem((chunks, groups, piece, width), BF16),
        maps=vmem((groups, piece, 2 * LANES), BF16),
        steps=vmem((groups, piece, heads), BF16),
        gmaps=vmem((groups, piece, 2 * LANES), BF16),
        gsteps=vmem((groups, piece, heads), BF16),
        sidef=vmem((seq, 3 * LANES), F32),
        og=vmem((3, seq, width), BF16),
        y=vmem((2, seq, width), BF16),
        x=vmem((2, seq, width), F32),
        gx=vmem((seq, width), F32),
        one=vmem((2, 2 * LANES, width), BF16),
        fresh=vmem((2, blocks, LANES, width), F32),
        dfresh=vmem((2, blocks, LANES, width), F32),
        state=vmem((blocks, LANES, width), BF16),
        dstate=vmem((blocks, LANES, width), BF16),
        run=vmem((LANES, width), F32),
        states=vmem((chunks, 2, LANES, width), BF16),
        around=vmem((chunks, slices, LANES, width), BF16),
        decays=vmem((slices, 8, LANES), F32),
        decay_own=vmem((8, LANES), F32),
        through=vmem((8, LANES), F32),
        through_wide=vmem((2, 8, width), F32),
        flow=vmem((8, LANES), F32),
        flow_wide=vmem((8, width), F32),
        mask=vmem((blocks, BLOCK, BLOCK), F32),
        scores=vmem((blocks, BLOCK, BLOCK), F32),
        dscores=vmem((blocks, BLOCK, BLOCK), F32),
        weight=vmem((blocks, BLOCK, BLOCK), F32),
        b_map=vmem((blocks, BLOCK, LANES), BF16),
        c_map=vmem((blocks, BLOCK, LANES), BF16),
        b_turned=vmem((blocks, LANES, BLOCK), BF16),
        c_turned=vmem((blocks, LANES, BLOCK), BF16),
        step=vmem((blocks, BLOCK, LANES), BF16),
        opening=vmem((blocks, BLOCK, 2 * LANES), BF16),
        tail=vmem((blocks, BLOCK, 2 * LANES), BF16),
        cum_col=vmem((blocks, chunks, BLOCK, CHUNK_HEADS), F32),
        cum_row=vmem((blocks, LANES, BLOCK), F32),
        dc=vmem((blocks, BLOCK, LANES), F32),
        db=vmem((blocks, BLOCK, LANES), F32),
        edge=vmem((blocks, BLOCK, LANES), F32),
        dstep=vmem((blocks, BLOCK, LANES), F32),
        side_send=dma((2,)), side_recv=dma((2,)), side_own=dma((2,)),
        gside_send=dma((2,)), gside_recv=dma((2,)), gside_own=dma((2,)),
        decay_send=dma((1,)), decay_recv=dma((1,)),
        val_send=dma((chunks,)), val_recv=dma((chunks,)), val_own=dma((chunks,)),
        gx_send=dma((chunks,)), gx_recv=dma((chunks,)), gx_own=dma((chunks,)),
        state_send=dma((chunks,)), state_recv=dma((chunks,)),
        og_sem=dma((3,)), y_sem=dma((2,)),
    )
    names = (
        "x_hbm", "maps_hbm", "steps_hbm", "og_hbm", "rate", "lens", "flags",
        "y_hbm", "gx_hbm", "gmaps_hbm", "gsteps_hbm",
    ) + tuple(scratch)
    anywhere = pl.BlockSpec(memory_space=pl.ANY)
    in_vmem = pl.BlockSpec(memory_space=pltpu.VMEM)
    in_smem = pl.BlockSpec(memory_space=pltpu.SMEM)
    y, gx, gmaps, gsteps = pl.pallas_call(
        partial(kernel, (groups, slices, piece, heads, size), names),
        out_shape=(
            pltpu.VMEM((seq, total), BF16),
            pltpu.VMEM((groups, piece, total), BF16),
            pltpu.VMEM((groups, piece, 2 * LANES), BF16),
            pltpu.VMEM((groups, piece, heads), BF16),
        ),
        in_specs=[anywhere] * 4 + [in_vmem, in_smem, in_smem],
        out_specs=[anywhere] * 4,
        scratch_shapes=list(scratch.values()),
        compiler_params=pltpu.CompilerParams(
            collective_id=0, has_side_effects=True, vmem_limit_bytes=47 * 1024 * 1024
        ),
        name="layer",
    )(
        inputs_load[0, 0],
        maps_load[0, 0],
        steps_load[0, 0],
        out_grad[0],
        decay_rate[None],
        doc_lengths,
        forget_flags,
    )
    held = tuple(
        pltpu.with_memory_space_constraint(a, pltpu.VMEM) for a in (y, gx, gmaps, gsteps)
    )
    y, gx, gmaps, gsteps = pl.pallas_call(
        hand_over,
        out_shape=tuple(jax.ShapeDtypeStruct(a.shape, a.dtype) for a in held),
        in_specs=[anywhere] * 4,
        out_specs=[anywhere] * 4,
        scratch_shapes=[dma((4, COPY_PARTS))],
        compiler_params=pltpu.CompilerParams(vmem_limit_bytes=1024 * 1024),
        name="hand_over",
    )(*held)
    return y[None], gx[None, None], gmaps[None, None], gsteps[None, None]


def solution(mesh):
    in_specs = (
        P("context", "group", None, None, None),
        P("context", "group", None, None, None),
        P("context", "group", None, None, None),
        P(),
        P("group", None),
        P("group", None),
        P("group", "context", None),
    )
    out_specs = (
        P("group", "context", None),
        P("context", "group", None, None, None),
        P("context", "group", None, None, None),
        P("context", "group", None, None, None),
    )
    return jax.shard_map(
        on_device, mesh=mesh, in_specs=in_specs, out_specs=out_specs, check_vma=False
    )
```

```python
from functools import partial
from types import SimpleNamespace

import jax
import jax.numpy as jnp
from jax import lax
from jax.experimental import pallas as pl
from jax.experimental.pallas import tpu as pltpu
from jax.sharding import PartitionSpec as P

BLOCK = 128
CHUNK_HEADS = 8
AHEAD = 3
LANES = 128
LOG2E = 1.4426950408889634
MESH = pl.DeviceIdType.MESH
F32 = jnp.float32
BF16 = jnp.bfloat16


def dot_nn(a, b):
    return jnp.dot(a, b, preferred_element_type=F32)


def dot_nt(a, b):
    return lax.dot_general(a, b, (((1,), (1,)), ((), ())), preferred_element_type=F32)


def dot_tn(a, b):
    return lax.dot_general(a, b, (((0,), (0,)), ((), ())), preferred_element_type=F32)


def dot_exact(a, b):
    return jnp.dot(a, b, precision=lax.Precision.HIGHEST, preferred_element_type=F32)


def halves(a):
    high = a.astype(BF16)
    return jnp.concatenate([high, (a - high.astype(F32)).astype(BF16)], axis=1)


def loop(count, body):
    def step(i, carry):
        body(i)
        return carry

    lax.fori_loop(0, count, step, 0)


def kernel(dims, names, *refs):
    r = SimpleNamespace(**dict(zip(names, refs)))
    groups, slices, piece, heads, size = dims
    seq = groups * piece
    blocks = seq // BLOCK
    chunks = heads // CHUNK_HEADS
    width = CHUNK_HEADS * size
    docs = r.lens.shape[1]
    me, place = lax.axis_index("group"), lax.axis_index("context")
    offset = place * seq

    def peer(i):
        return lax.rem(me + i, groups)

    turns = ((0, 1), (1, 0), (0, 3), (3, 0), (0, 2), (2, 0), (1, 1), (3, 3), (1, 3), (3, 1))
    turns += ((2, 2), (1, 2), (2, 1), (3, 2), (2, 3))

    def others():
        if groups != 32:
            return [peer(i) for i in range(1, groups)]
        core, z, y = lax.rem(me, 2), lax.rem(me // 2, 4), me // 8
        found = []
        for other in (0, 1):
            for dy, dz in turns:
                chip = lax.rem(y + dy, 4) * 4 + lax.rem(z + dz, 4)
                found.append(chip * 2 + lax.rem(core + other, 2))
        return found + [me + 1 - 2 * core]

    def ctx(i):
        return lax.rem(place + i, slices)

    def rows(b):
        return pl.ds(pl.multiple_of(b * BLOCK, BLOCK), BLOCK)

    def cols(k):
        return pl.ds(pl.multiple_of(k * width, width), width)

    def piece_rows(j):
        return pl.ds(pl.multiple_of(j * piece, 8), piece)

    def to_group(src, dst, send, recv, j):
        return pltpu.make_async_remote_copy(
            src_ref=src, dst_ref=dst, send_sem=send, recv_sem=recv,
            device_id={"group": j}, device_id_type=MESH,
        )

    def to_context(src, dst, send, recv, c):
        return pltpu.make_async_remote_copy(
            src_ref=src, dst_ref=dst, send_sem=send, recv_sem=recv,
            device_id={"context": c}, device_id_type=MESH,
        )

    def take(ref, sem):
        pltpu.make_async_copy(ref, ref, sem).wait()

    barrier = pltpu.get_barrier_semaphore()

    def greet_group(i):
        pl.semaphore_signal(barrier, inc=1, device_id={"group": peer(i + 1)}, device_id_type=MESH)

    def greet_context(i):
        pl.semaphore_signal(barrier, inc=1, device_id={"context": ctx(i + 1)}, device_id_type=MESH)

    loop(groups - 1, greet_group)
    loop(slices - 1, greet_context)
    pl.semaphore_wait(barrier, groups + slices - 2)

    side_refs = ((r.maps_hbm, r.maps), (r.steps_hbm, r.steps))

    def send_side(j):
        for n, (source, target) in enumerate(side_refs):
            to_group(
                source.at[j], target.at[me], r.side_send.at[n], r.side_recv.at[n], j
            ).start()

    def own_side():
        return [
            pltpu.make_async_copy(source.at[me], target.at[me], r.side_own.at[n])
            for n, (source, target) in enumerate(side_refs)
        ]

    def send_values(k):
        for j in others():
            to_group(
                r.x_hbm.at[j, :, cols(k)], r.vals.at[k, me], r.val_send.at[k], r.val_recv.at[k], j
            ).start()
        own_values(k).start()

    def own_values(k):
        return pltpu.make_async_copy(
            r.x_hbm.at[me, :, cols(k)], r.vals.at[k, me], r.val_own.at[k]
        )

    def load_grad(k):
        slot = lax.rem(k, 3)
        return pltpu.make_async_copy(r.og_hbm.at[:, cols(k)], r.og.at[slot], r.og_sem.at[slot])

    def store_out(k):
        slot = lax.rem(k, 2)
        return pltpu.make_async_copy(r.y.at[slot], r.y_hbm.at[:, cols(k)], r.y_sem.at[slot])

    for j in others():
        send_side(j)
    for copy in own_side():
        copy.start()
    loop(min(AHEAD, chunks), send_values)
    load_grad(0).start()

    for n, (_, target) in enumerate(side_refs):
        take(target.at[pl.ds(0, groups - 1)], r.side_recv.at[n])
    for copy in own_side():
        copy.wait()
    step_at = slice(2 * LANES, 2 * LANES + heads)
    r.sidef[:, 2 * LANES :] = jnp.zeros((seq, LANES), F32)

    def unpack_side(j):
        r.sidef[piece_rows(j), : 2 * LANES] = r.maps[j].astype(F32)
        r.sidef[piece_rows(j), step_at] = r.steps[j].astype(F32)

    loop(groups, unpack_side)

    ends = [r.lens[0, 0]]
    for d in range(1, docs):
        ends.append(ends[-1] + r.lens[0, d])

    def segment(position):
        return sum(jnp.where(position >= end, 1, 0) for end in ends)

    row_at = lax.broadcasted_iota(jnp.int32, (BLOCK, BLOCK), 0)
    col_at = lax.broadcasted_iota(jnp.int32, (BLOCK, BLOCK), 1)
    rate = r.rate[...]
    if heads < LANES:
        rate = jnp.concatenate([rate, jnp.zeros((1, LANES - heads), F32)], axis=1)

    def block_segments(b):
        first = offset + b * BLOCK
        before = jnp.where(first > 0, segment(first - 1), -1)
        last = segment(first + BLOCK - 1)
        return segment(first + row_at), segment(first + col_at), before, last

    def prepare(b):
        seg_row, seg_col, before, last = block_segments(b)
        kept = (seg_row == seg_col) & (row_at >= col_at)
        r.mask[b] = jnp.where(kept, 0.0, -1e30)
        part = r.sidef[rows(b), :]
        b_map, c_map, step = part[:, :LANES], part[:, LANES : 2 * LANES], part[:, 2 * LANES :]
        b_part, c_part = b_map.astype(BF16), c_map.astype(BF16)
        r.b_map[b], r.c_map[b] = b_part, c_part
        r.b_turned[b], r.c_turned[b] = b_map.T.astype(BF16), c_map.T.astype(BF16)
        r.scores[b] = dot_nt(c_part, b_part)
        r.step[b] = step.astype(BF16)
        lower = jnp.where(row_at >= col_at, 1.0, 0.0)
        cum = dot_exact(lower, step * (rate * -LOG2E))
        end = cum[BLOCK - 1 : BLOCK, :]
        r.opening[b] = halves(jnp.where(seg_row == before, jnp.exp2(cum), 0.0))
        r.tail[b] = halves(jnp.where(seg_row == last, jnp.exp2(end - cum), 0.0))
        r.through[pl.ds(b, 1), :] = jnp.where(last == before, jnp.exp2(end), 0.0)
        for k in range(chunks):
            r.cum_col[b, k] = cum[:, k * CHUNK_HEADS : (k + 1) * CHUNK_HEADS]
        r.cum_row[b] = cum.T
        picked = sum(jnp.where(seg_row == d, r.flags[0, d], 0) for d in range(docs))
        r.weight[b] = 1.0 - 1.5 * picked.astype(F32)
        r.dscores[b] = jnp.zeros((BLOCK, BLOCK), F32)
        for name in ("dc", "db", "edge", "dstep"):
            getattr(r, name)[b] = jnp.zeros((BLOCK, LANES), F32)

    r.through[...] = jnp.ones(r.through.shape, F32)
    r.flow[...] = jnp.zeros(r.flow.shape, F32)
    loop(blocks, prepare)

    decay = r.through[0:1, :]
    for b in range(1, blocks):
        decay = decay * r.through[b : b + 1, :]
    r.decay_own[...] = jnp.broadcast_to(decay, r.decay_own.shape)

    def send_decay(i):
        c = ctx(i + 1)
        to_context(
            r.decay_own, r.decays.at[place], r.decay_send.at[0], r.decay_recv.at[0], c
        ).start()

    loop(slices - 1, send_decay)
    take(r.decays.at[pl.ds(0, slices - 1)], r.decay_recv.at[0])
    take(r.decays.at[pl.ds(0, slices - 1)], r.decay_send.at[0])

    def spread(k):
        head = lax.broadcasted_iota(jnp.int32, (LANES, width), 0)
        col = lax.broadcasted_iota(jnp.int32, (LANES, width), 1)
        low = (head - k * CHUNK_HEADS) * size
        return jnp.where((col >= low) & (col < low + size), 1.0, 0.0).astype(BF16)

    def first_half(k):
        slot, held = lax.rem(k, 2), lax.rem(k, 3)
        take(r.vals.at[k, pl.ds(0, groups - 1)], r.val_recv.at[k])
        own_values(k).wait()
        load_grad(k).wait()

        def unpack(j):
            r.x[slot, piece_rows(j), :] = r.vals[k, j].astype(F32)

        loop(groups, unpack)
        one = spread(k)
        r.one[slot, pl.ds(0, LANES)] = one
        r.one[slot, pl.ds(LANES, LANES)] = one
        r.through_wide[slot] = dot_nn(halves(r.through[...]), r.one[slot])
        r.run[...] = jnp.zeros(r.run.shape, F32)

        def fresh(b):
            both = r.one[slot]
            step = dot_nn(r.step[b], both[:LANES])
            tail = dot_nn(r.tail[b], both)
            scaled = (r.x[slot, rows(b), :] * step * tail).astype(BF16)
            r.fresh[slot, b] = dot_nn(r.b_turned[b], scaled)
            through = r.through_wide[slot, pl.ds(b, 1), :]
            r.run[...] = through * r.run[...] + r.fresh[slot, b]
            opening = dot_nn(r.opening[b], both)
            grad = r.og[held, rows(b), :].astype(F32) * r.weight[b][:, :1]
            r.og[held, rows(b), :] = grad.astype(BF16)
            r.dfresh[slot, b] = dot_nn(r.c_turned[b], (grad * opening).astype(BF16))

        loop(blocks, fresh)
        r.states[k, 0] = r.run[...].astype(BF16)
        r.run[...] = jnp.zeros(r.run.shape, F32)

        def back(turn):
            b = blocks - 1 - turn
            through = r.through_wide[slot, pl.ds(b, 1), :]
            r.run[...] = through * r.run[...] + r.dfresh[slot, b]

        loop(blocks, back)
        r.states[k, 1] = r.run[...].astype(BF16)

        def send_state(i):
            c = ctx(i + 1)
            kind = jnp.where(c > place, 0, 1)
            to_context(
                r.states.at[k, kind], r.around.at[k, place], r.state_send.at[k], r.state_recv.at[k], c
            ).start()

        loop(slices - 1, send_state)

    def second_half(k):
        slot, held = lax.rem(k, 2), lax.rem(k, 3)
        take(r.around.at[k, pl.ds(0, slices - 1)], r.state_recv.at[k])

        def widened(c):
            return dot_nn(halves(r.decays[c]), r.one[slot])[:1]

        r.run[...] = jnp.zeros(r.run.shape, F32)

        def enter(c):
            @pl.when(c < place)
            def _():
                r.run[...] = r.around[k, c].astype(F32) + widened(c) * r.run[...]

        loop(slices, enter)

        def forward(b):
            r.state[b] = r.run[...].astype(BF16)
            through = r.through_wide[slot, pl.ds(b, 1), :]
            new = through * r.run[...] + r.fresh[slot, b]
            r.run[...] = new
            r.fresh[slot, b] = new

        loop(blocks, forward)
        r.run[...] = jnp.zeros(r.run.shape, F32)

        def leave(turn):
            c = slices - 1 - turn

            @pl.when(c > place)
            def _():
                r.run[...] = r.around[k, c].astype(F32) + widened(c) * r.run[...]

        loop(slices, leave)
        r.flow_wide[...] = jnp.zeros(r.flow_wide.shape, F32)

        def backward(turn):
            b = blocks - 1 - turn
            now = r.run[...]
            r.dstate[b] = now.astype(BF16)
            r.flow_wide[pl.ds(b, 1), :] = jnp.sum(now * r.fresh[slot, b], axis=0, keepdims=True)
            through = r.through_wide[slot, pl.ds(b, 1), :]
            r.run[...] = through * now + r.dfresh[slot, b]

        loop(blocks, backward)
        one = r.one[slot, pl.ds(0, LANES)]

        def per_head(a):
            high = a.astype(BF16)
            low = (a - high.astype(F32)).astype(BF16)
            return dot_nt(high, one) + dot_nt(low, one)

        r.flow[...] += per_head(r.flow_wide[...])

        @pl.when(k >= 2)
        def _():
            store_out(k - 2).wait()

        lane = lax.broadcasted_iota(jnp.int32, (1, LANES), 1)
        left = jnp.where(lane < size, 1.0, 0.0).astype(BF16)
        right = jnp.where(lane < size, 0.0, 1.0).astype(BF16)

        def block(b):
            both = r.one[slot]
            x = r.x[slot, rows(b), :]
            step = dot_nn(r.step[b], both[:LANES])
            tail = dot_nn(r.tail[b], both)
            opening = dot_nn(r.opening[b], both)
            grad = r.og[held, rows(b), :]
            stepped = x * step
            xd = stepped.astype(BF16)
            state, dstate = r.state[b], r.dstate[b]
            carried = dot_nn(r.c_map[b], state) * opening
            r.dc[b] += dot_nt((grad.astype(F32) * opening).astype(BF16), state)
            r.db[b] += dot_nt((stepped * tail).astype(BF16), dstate)
            dtail = dot_nn(r.b_map[b], dstate) * tail
            mask, scores = r.mask[b], r.scores[b]
            cum_row = r.cum_row[b, pl.ds(pl.multiple_of(k * CHUNK_HEADS, 8), CHUNK_HEADS), :]
            cum_col = r.cum_col[b, k]
            dscores = r.dscores[b]
            ys, dxs = [], []
            for p in range(width // LANES):
                at = slice(p * LANES, (p + 1) * LANES)
                xp, gp = xd[:, at], grad[:, at]
                x_two = jnp.concatenate([xp * left, xp * right], axis=0)
                g_two = jnp.concatenate([gp * left, gp * right], axis=0)
                dmixing = dot_nt(gp, x_two)
                mixing = []
                for q in range(2):
                    h = 2 * p + q
                    fade = jnp.exp2(cum_col[:, h : h + 1] - cum_row[h : h + 1, :] + mask)
                    mixing.append((fade * scores).astype(BF16))
                    dscores = dscores + dmixing[:, q * BLOCK : (q + 1) * BLOCK] * fade
                ys.append(dot_nn(jnp.concatenate(mixing, axis=1), x_two))
                dxs.append(dot_tn(jnp.concatenate(mixing, axis=0), g_two))
            r.dscores[b] = dscores
            y = jnp.concatenate(ys, axis=1) + carried
            dxd = jnp.concatenate(dxs, axis=1) + dtail
            r.y[slot, rows(b), :] = y.astype(BF16)
            r.gx[rows(b), :] = dxd * step
            r.edge[b] += per_head(grad.astype(F32) * y - xd.astype(F32) * dxd)
            r.dstep[b] += per_head(x * dxd)

        loop(blocks, block)
        store_out(k).start()

        def pack(j):
            r.gsend[k, j] = r.gx[piece_rows(j), :].astype(BF16)

        for j in others():
            pack(j)
            to_group(
                r.gsend.at[k, j], r.gx_hbm.at[me, :, cols(k)], r.gx_send.at[k], r.gx_recv.at[k], j
            ).start()
        pack(me)
        own_gradient(k).start()

    def own_gradient(k):
        return pltpu.make_async_copy(
            r.gsend.at[k, me], r.gx_hbm.at[me, :, cols(k)], r.gx_own.at[k]
        )

    def turn(k):
        @pl.when(k + AHEAD < chunks)
        def _():
            send_values(k + AHEAD)

        @pl.when(k < chunks)
        def _():
            @pl.when(k + 1 < chunks)
            def _():
                load_grad(k + 1).start()

            first_half(k)

        @pl.when(k > 0)
        def _():
            second_half(k - 1)

    loop(chunks + 1, turn)

    def finish(b):
        seg_row, seg_col, before, last = block_segments(b)
        dscores = r.dscores[b].astype(BF16)
        later = jnp.where((seg_row == seg_col) & (col_at >= row_at), 1.0, 0.0)
        dlog = dot_exact(later, r.edge[b])
        dlog = dlog + jnp.where(seg_row == last, r.flow[pl.ds(b, 1), :], 0.0)
        r.sidef[rows(b), pl.ds(0, LANES)] = r.db[b] + dot_tn(dscores, r.c_map[b])
        r.sidef[rows(b), pl.ds(LANES, LANES)] = r.dc[b] + dot_nn(dscores, r.b_map[b])
        r.sidef[rows(b), pl.ds(2 * LANES, LANES)] = r.dstep[b] - rate * dlog

    loop(blocks, finish)

    gside_refs = ((r.gmaps, r.gmaps_hbm), (r.gsteps, r.gsteps_hbm))

    def pack_side(j):
        r.gmaps[j] = r.sidef[piece_rows(j), : 2 * LANES].astype(BF16)
        r.gsteps[j] = r.sidef[piece_rows(j), step_at].astype(BF16)

    for j in others():
        pack_side(j)
        for n, (source, target) in enumerate(gside_refs):
            to_group(
                source.at[j], target.at[me], r.gside_send.at[n], r.gside_recv.at[n], j
            ).start()
    pack_side(me)
    own = [
        pltpu.make_async_copy(source.at[me], target.at[me], r.gside_own.at[n])
        for n, (source, target) in enumerate(gside_refs)
    ]
    for copy in own:
        copy.start()

    def settle(k):
        take(r.vals.at[k, pl.ds(0, groups - 1)], r.val_send.at[k])
        take(r.around.at[k, pl.ds(0, slices - 1)], r.state_send.at[k])
        take(r.vals.at[k, pl.ds(0, groups - 1)], r.gx_send.at[k])
        take(r.vals.at[k, pl.ds(0, groups - 1)], r.gx_recv.at[k])
        own_gradient(k).wait()

    loop(chunks, settle)
    for k in range(max(chunks - 2, 0), chunks):
        store_out(k).wait()
    for copy in own:
        copy.wait()
    for sem in (r.side_send, r.gside_send, r.gside_recv):
        for n, (_, like) in enumerate(side_refs):
            take(like.at[pl.ds(0, groups - 1)], sem.at[n])


COPY_PARTS = 8


def hand_over(*refs):
    count = len(refs) // 2
    sems = refs[-1]
    copies = []
    for n, (source, target) in enumerate(zip(refs[:count], refs[count : 2 * count])):
        parts = COPY_PARTS if source.shape[-1] > 2 * LANES else 1
        length = source.shape[0] // parts
        for p in range(parts):
            at = pl.ds(p * length, length)
            copies.append(pltpu.make_async_copy(source.at[at], target.at[at], sems.at[n, p]))
    for copy in copies:
        copy.start()
    for copy in copies:
        copy.wait()


def on_device(inputs_load, maps_load, steps_load, decay_rate, doc_lengths, forget_flags, out_grad):
    groups, slices = lax.axis_size("group"), lax.axis_size("context")
    heads = decay_rate.shape[0]
    piece, total = inputs_load.shape[3:]
    size = total // heads
    seq = groups * piece
    blocks = seq // BLOCK
    chunks = heads // CHUNK_HEADS
    width = CHUNK_HEADS * size

    dma = pltpu.SemaphoreType.DMA
    vmem = pltpu.VMEM
    scratch = dict(
        vals=vmem((chunks, groups, piece, width), BF16),
        gsend=vmem((chunks, groups, piece, width), BF16),
        maps=vmem((groups, piece, 2 * LANES), BF16),
        steps=vmem((groups, piece, heads), BF16),
        gmaps=vmem((groups, piece, 2 * LANES), BF16),
        gsteps=vmem((groups, piece, heads), BF16),
        sidef=vmem((seq, 3 * LANES), F32),
        og=vmem((3, seq, width), BF16),
        y=vmem((2, seq, width), BF16),
        x=vmem((2, seq, width), F32),
        gx=vmem((seq, width), F32),
        one=vmem((2, 2 * LANES, width), BF16),
        fresh=vmem((2, blocks, LANES, width), F32),
        dfresh=vmem((2, blocks, LANES, width), F32),
        state=vmem((blocks, LANES, width), BF16),
        dstate=vmem((blocks, LANES, width), BF16),
        run=vmem((LANES, width), F32),
        states=vmem((chunks, 2, LANES, width), BF16),
        around=vmem((chunks, slices, LANES, width), BF16),
        decays=vmem((slices, 8, LANES), F32),
        decay_own=vmem((8, LANES), F32),
        through=vmem((8, LANES), F32),
        through_wide=vmem((2, 8, width), F32),
        flow=vmem((8, LANES), F32),
        flow_wide=vmem((8, width), F32),
        mask=vmem((blocks, BLOCK, BLOCK), F32),
        scores=vmem((blocks, BLOCK, BLOCK), F32),
        dscores=vmem((blocks, BLOCK, BLOCK), F32),
        weight=vmem((blocks, BLOCK, BLOCK), F32),
        b_map=vmem((blocks, BLOCK, LANES), BF16),
        c_map=vmem((blocks, BLOCK, LANES), BF16),
        b_turned=vmem((blocks, LANES, BLOCK), BF16),
        c_turned=vmem((blocks, LANES, BLOCK), BF16),
        step=vmem((blocks, BLOCK, LANES), BF16),
        opening=vmem((blocks, BLOCK, 2 * LANES), BF16),
        tail=vmem((blocks, BLOCK, 2 * LANES), BF16),
        cum_col=vmem((blocks, chunks, BLOCK, CHUNK_HEADS), F32),
        cum_row=vmem((blocks, LANES, BLOCK), F32),
        dc=vmem((blocks, BLOCK, LANES), F32),
        db=vmem((blocks, BLOCK, LANES), F32),
        edge=vmem((blocks, BLOCK, LANES), F32),
        dstep=vmem((blocks, BLOCK, LANES), F32),
        side_send=dma((2,)), side_recv=dma((2,)), side_own=dma((2,)),
        gside_send=dma((2,)), gside_recv=dma((2,)), gside_own=dma((2,)),
        decay_send=dma((1,)), decay_recv=dma((1,)),
        val_send=dma((chunks,)), val_recv=dma((chunks,)), val_own=dma((chunks,)),
        gx_send=dma((chunks,)), gx_recv=dma((chunks,)), gx_own=dma((chunks,)),
        state_send=dma((chunks,)), state_recv=dma((chunks,)),
        og_sem=dma((3,)), y_sem=dma((2,)),
    )
    names = (
        "x_hbm", "maps_hbm", "steps_hbm", "og_hbm", "rate", "lens", "flags",
        "y_hbm", "gx_hbm", "gmaps_hbm", "gsteps_hbm",
    ) + tuple(scratch)
    anywhere = pl.BlockSpec(memory_space=pl.ANY)
    in_vmem = pl.BlockSpec(memory_space=pltpu.VMEM)
    in_smem = pl.BlockSpec(memory_space=pltpu.SMEM)
    y, gx, gmaps, gsteps = pl.pallas_call(
        partial(kernel, (groups, slices, piece, heads, size), names),
        out_shape=(
            pltpu.VMEM((seq, total), BF16),
            pltpu.VMEM((groups, piece, total), BF16),
            pltpu.VMEM((groups, piece, 2 * LANES), BF16),
            pltpu.VMEM((groups, piece, heads), BF16),
        ),
        in_specs=[anywhere] * 4 + [in_vmem, in_smem, in_smem],
        out_specs=[anywhere] * 4,
        scratch_shapes=list(scratch.values()),
        compiler_params=pltpu.CompilerParams(
            collective_id=0, has_side_effects=True, vmem_limit_bytes=47 * 1024 * 1024
        ),
        name="layer",
    )(
        inputs_load[0, 0],
        maps_load[0, 0],
        steps_load[0, 0],
        out_grad[0],
        decay_rate[None],
        doc_lengths,
        forget_flags,
    )
    held = tuple(
        pltpu.with_memory_space_constraint(a, pltpu.VMEM) for a in (y, gx, gmaps, gsteps)
    )
    y, gx, gmaps, gsteps = pl.pallas_call(
        hand_over,
        out_shape=tuple(jax.ShapeDtypeStruct(a.shape, a.dtype) for a in held),
        in_specs=[anywhere] * 4,
        out_specs=[anywhere] * 4,
        scratch_shapes=[dma((4, COPY_PARTS))],
        compiler_params=pltpu.CompilerParams(vmem_limit_bytes=1024 * 1024),
        name="hand_over",
    )(*held)
    return y[None], gx[None, None], gmaps[None, None], gsteps[None, None]


def solution(mesh):
    in_specs = (
        P("context", "group", None, None, None),
        P("context", "group", None, None, None),
        P("context", "group", None, None, None),
        P(),
        P("group", None),
        P("group", None),
        P("group", "context", None),
    )
    out_specs = (
        P("group", "context", None),
        P("context", "group", None, None, None),
        P("context", "group", None, None, None),
        P("context", "group", None, None, None),
    )
    return jax.shard_map(
        on_device, mesh=mesh, in_specs=in_specs, out_specs=out_specs, check_vma=False
    )
```
